512 devices in a mesh: cells: 8 (over x, y_lo), dp: 64 (over y_hi, z, core).
Axes of the slice: x: 4, y: 8 (y_hi: 4, y_lo: 2; y = y_hi * 2 + y_lo), z: 8, core: 2. Of those that a mesh axis runs over, the one named last changes fastest.
Arguments:
- sensitivity: bfloat16 [16384, 8192], P('dp', 'cells'), may hold values from -6 to 6
- weights: float32 [16384], P('dp'), may hold values from 0.3 to 3
- coef_x: float32 [8192], P('cells'), may hold values from 0.04 to 0.16
- coef_y: float32 [8192], P('cells'), may hold values from 0.04 to 0.16
- coef_z: float32 [8192], P('cells'), may hold values from 0.04 to 0.16
Outputs:
- gram: float32 [16384, 1024], P('dp', 'cells')
The draws below stay inside these ranges and needn't reach their ends.
All inputs are finite; a program needn't handle non-finite values.
Results may differ from the reference program's by a relative error of at most 0.00092.
Values may be sent and summed in bfloat16 or wider, within the bound.
A program may use at most 64 MiB of HBM per device.

```python
import math
import jax
import jax.numpy as jnp
from jax import lax

ROWS_DEV = 256
CY = 4
CZ = 128
BAND = 3
SMOOTH = 2
NX = 16
NCELLS = 8192
NDATA = 16384


def steps_of(stream_key, extent, cuts, smallest, top_value):
    loudness = 1.0
    for position, shards_of in cuts:
        heights = jax.random.uniform(jax.random.fold_in(jax.random.fold_in(stream_key, 6), position), (shards_of,), jnp.float32, smallest / len(cuts), top_value / len(cuts))
        loudness = loudness * jnp.repeat(jnp.exp(heights), extent[position] // shards_of).reshape((-1,) + (1,) * (len(extent) - 1 - position))
    return loudness


def scatter_about(stream_key, shape, scale, limit, cuts=(), kind=jnp.bfloat16):
    level = steps_of(stream_key, shape, cuts, -0.22, 0.18) if cuts else 1.0
    drawn = jax.random.normal(stream_key, shape, jnp.float32) * scale * level
    return jnp.minimum(jnp.maximum(drawn, -limit), limit).astype(kind)


def setup_inputs(seed: int = 0) -> dict:
    arg_keys = jax.random.split(jax.random.key(seed), 6)
    sensitivity = scatter_about(arg_keys[0], (NDATA, NCELLS), 1.0, 6.0, ((0, 64), (1, 8)))
    weights = jnp.clip(jnp.exp(math.log(3.0) - 2.3025851 * jax.random.uniform(arg_keys[1], (NDATA,), jnp.float32) ** steps_of(arg_keys[1], (NDATA,), ((0, 64),), -0.2, 0.2)), 0.3, 3.0)
    coef_x = jnp.clip(jnp.exp(math.log(0.16) - 1.3862944 * jax.random.uniform(arg_keys[2], (NCELLS,), jnp.float32) ** steps_of(arg_keys[2], (NCELLS,), ((0, 8),), -0.2, 0.2)), 0.04, 0.16)
    coef_y = jnp.clip(jnp.exp(math.log(0.16) - 1.3862944 * jax.random.uniform(arg_keys[3], (NCELLS,), jnp.float32) ** steps_of(arg_keys[3], (NCELLS,), ((0, 8),), -0.2, 0.2)), 0.04, 0.16)
    coef_z = jnp.clip(jnp.exp(math.log(0.16) - 1.3862944 * jax.random.uniform(arg_keys[4], (NCELLS,), jnp.float32) ** steps_of(arg_keys[4], (NCELLS,), ((0, 8),), -0.2, 0.2)), 0.04, 0.16)
    return dict(sensitivity=sensitivity, weights=weights, coef_x=coef_x, coef_y=coef_y, coef_z=coef_z)


def face_term(field, coef, axis):
    length = field.shape[axis]
    diff = lax.slice_in_dim(field, 1, length, axis=axis) - lax.slice_in_dim(field, 0, length - 1, axis=axis)
    flux = lax.slice_in_dim(coef, 0, length - 1, axis=axis - 1) * diff
    upper = [(0, 0)] * field.ndim
    lower = [(0, 0)] * field.ndim
    upper[axis] = (0, 1)
    lower[axis] = (1, 0)
    return jnp.pad(flux, upper) - jnp.pad(flux, lower)


def reference(sensitivity, weights, coef_x, coef_y, coef_z):
    blocks_count = NDATA // ROWS_DEV
    grid_x = coef_x.reshape(NX, CY, CZ)
    grid_y = coef_y.reshape(NX, CY, CZ)
    grid_z = coef_z.reshape(NX, CY, CZ)
    blocks = sensitivity.reshape(blocks_count, ROWS_DEV, NX, CY, CZ)
    weight_blocks = weights.reshape(blocks_count, ROWS_DEV)

    def make_panel(pair):
        rows, weight_rows = pair
        field = rows.astype(jnp.float32)
        for step in range(SMOOTH):
            change = face_term(field, grid_x, 1) + face_term(field, grid_y, 2) + face_term(field, grid_z, 3)
            field = field + change
        return (weight_rows[:, None, None, None] * field).astype(jnp.bfloat16).reshape(ROWS_DEV, NCELLS)

    panels = lax.map(make_panel, (blocks, weight_blocks))
    scale = float(NCELLS) ** -0.5

    def tiles(block):
        own = lax.dynamic_index_in_dim(panels, block, 0, keepdims=False)
        pieces = []
        for offset in range(BAND + 1):
            other_index = ((block + offset) % blocks_count).astype(jnp.int32)
            other = lax.dynamic_index_in_dim(panels, other_index, 0, keepdims=False)
            product = lax.dot_general(own, other, (((1,), (1,)), ((), ())), preferred_element_type=jnp.float32)
            pieces.append(product * scale)
        return jnp.concatenate(pieces, axis=1)

    gram = lax.map(tiles, jnp.arange(blocks_count, dtype=jnp.int32))
    return gram.reshape(NDATA, (BAND + 1) * ROWS_DEV)
```

```python
import functools

import jax
import jax.numpy as jnp
from jax import lax
from jax.experimental import pallas as pl
from jax.experimental.pallas import tpu as pltpu
from jax.sharding import PartitionSpec as P

CY = 4
CZ = 128
GROUP = 16
MESH = pl.DeviceIdType.MESH
PANEL = 3


def smoothing_pass(load, coef, store):
    def step(part, carry):
        current, entering = carry
        for half in range(2):
            if half == 0:
                above = [load(part, CY + y) for y in range(CY)]
            else:
                upper = jnp.minimum(part + 1, 7)
                above = [load(upper, y) for y in range(CY)]
            flux_x = []
            below_y = None
            for y in range(CY):
                row = half * CY + y
                here = current[y]
                flux = coef[part, pl.ds(row, 1), :] * (above[y] - here)
                change = flux - entering[y]
                flux_x.append(flux)
                if y < CY - 1:
                    flux_y = coef[part, pl.ds(8 + row, 1), :] * (current[y + 1] - here)
                    change = change + flux_y
                if y > 0:
                    change = change - below_y
                below_y = flux_y
                flux_z = coef[part, pl.ds(16 + row, 1), :] * (pltpu.roll(here, CZ - 1, 1) - here)
                change = change + (flux_z - pltpu.roll(flux_z, 1, 1))
                store(part, row, here + change)
            current, entering = tuple(above), tuple(flux_x)
        return current, entering

    first = tuple(load(0, y) for y in range(CY))
    zero = tuple(jnp.zeros((GROUP, CZ), jnp.float32) for _ in range(CY))
    lax.fori_loop(0, 8, step, (first, zero))


def kernel(
    scale, sens, weights_hbm, coef_x, coef_y, coef_z, out,
    weights, gathered, coef, slab_in, field, slab_out, panels, tiles, sums, last_out, last_in,
    coef_send, coef_recv, in_send, in_recv, own_sem, out_send, out_recv,
    a_send, b_send, c_send, panel_recv, tile_send, tile_recv, last_send, last_recv,
):
    c = lax.axis_index("cells")
    d = lax.axis_index("dp")
    blocks = lax.axis_size("dp")
    odd = lax.rem(d, 2)
    even = odd == 0
    rows = sens.shape[0] // 8

    def block(offset):
        return lax.rem(d + offset + blocks, blocks)

    def peer(j):
        return lax.rem(c + j, 8)

    def at_rows(index):
        return pl.ds(pl.multiple_of(index * rows, rows), rows)

    mine = jnp.logical_or(c < 4, jnp.logical_and(even, c < 6))

    barrier = pltpu.get_barrier_semaphore()

    def greet(cells, dp):
        pl.semaphore_signal(barrier, inc=1, device_id=(cells, dp), device_id_type=MESH)

    for j in range(1, 8):
        greet(peer(j), d)

    @pl.when(even)
    def _():
        greet(c, block(1))
        greet(c, block(2))

        @pl.when(c >= 6)
        def _():
            for j in range(1, 8):
                greet(peer(j), block(1))

    @pl.when(odd == 1)
    def _():
        greet(c, block(-1))
        greet(c, block(-2))
        greet(c, block(-3))

        @pl.when(c >= 4)
        def _():
            greet(c, block(2))

    own = [
        pltpu.make_async_copy(source, target, own_sem.at[i])
        for i, (source, target) in enumerate(
            [
                (coef_x, gathered.at[c, pl.ds(0, 8), :]),
                (coef_y, gathered.at[c, pl.ds(8, 8), :]),
                (coef_z, gathered.at[c, pl.ds(16, 8), :]),
                (weights_hbm, weights),
                (sens.at[at_rows(c), :], slab_in.at[c]),
            ]
        )
    ]
    for one in own:
        one.start()

    to_odd = 11 - (c >= 6).astype(jnp.int32) + (c >= 4).astype(jnp.int32)
    pl.semaphore_wait(barrier, jnp.where(even, 10, to_odd))

    def copy(source, target, send, recv, cells, dp):
        return pltpu.make_async_remote_copy(
            src_ref=source, dst_ref=target, send_sem=send, recv_sem=recv,
            device_id=(cells, dp), device_id_type=MESH,
        )

    def coef_copy(j):
        return copy(
            gathered.at[c], gathered.at[c], coef_send.at[j - 1], coef_recv.at[c], peer(j), d
        )

    def in_copy(j):
        to = peer(j)
        return copy(sens.at[at_rows(to), :], slab_in.at[c], in_send.at[j - 1], in_recv.at[c], to, d)

    for one in own[:3]:
        one.wait()
    for j in range(1, 8):
        coef_copy(j).start()
    for j in range(1, 8):
        in_copy(j).start()

    own[3].wait()
    lane = lax.broadcasted_iota(jnp.int32, (rows, CZ), 1)
    line = lax.broadcasted_iota(jnp.int32, (rows, CZ), 0)
    weight_row = jnp.where(c < 4, weights[0:1, :], weights[1:2, :])
    chosen = lane == line + lax.rem(c, 4) * rows
    weight = jnp.sum(jnp.where(chosen, weight_row, 0.0), axis=1, keepdims=True)

    def arrived(buffer, sem, s):
        return copy(buffer.at[s], buffer.at[s], sem.at[s], sem.at[s], c, d)

    for j in range(1, 8):
        arrived(gathered, coef_recv, peer(j)).wait_recv()
    inner = lax.broadcasted_iota(jnp.int32, (8, CZ), 1) < CZ - 1
    for s in range(8):
        if s < 7:
            coef[s, 0:8, :] = gathered[s, 0:8, :]
        else:
            coef[s, 0:4, :] = gathered[s, 0:4, :]
            coef[s, 4:8, :] = jnp.zeros((4, CZ), jnp.float32)
        coef[s, 8:16, :] = gathered[s, 8:16, :]
        coef[s, 16:24, :] = jnp.where(inner, gathered[s, 16:24, :], 0.0)
    own[4].wait()
    for j in range(1, 8):
        arrived(slab_in, in_recv, peer(j)).wait_recv()

    for group in range(rows // GROUP):
        part_rows = pl.ds(group * GROUP, GROUP)
        scaled = weight[group * GROUP : (group + 1) * GROUP]

        def load_in(part, tile, part_rows=part_rows):
            return slab_in[part, part_rows, pl.ds(tile * CZ, CZ)].astype(jnp.float32)

        def store_field(part, tile, value, part_rows=part_rows):
            field[part, part_rows, pl.ds(tile * CZ, CZ)] = value

        def load_field(part, tile, part_rows=part_rows):
            return field[part, part_rows, pl.ds(tile * CZ, CZ)]

        def store_out(part, tile, value, part_rows=part_rows, scaled=scaled):
            slab_out[part, part_rows, pl.ds(tile * CZ, CZ)] = (scaled * value).astype(jnp.bfloat16)

        smoothing_pass(load_in, coef, store_field)
        smoothing_pass(load_field, coef, store_out)

    def out_copy(j):
        to = peer(j)
        return copy(
            slab_out.at[to], panels.at[PANEL, at_rows(c), :], out_send.at[j - 1], out_recv.at[c], to, d
        )

    for j in range(1, 8):
        out_copy(j).start()
    panels[PANEL, at_rows(c), :] = slab_out[c]

    first_to = jnp.where(even, block(-2), block(-1))
    first_slot = jnp.where(even, 1, 0)
    second_to = jnp.where(even, block(3), block(2))
    second_slot = jnp.where(even, 2, 0)

    def piece(slot, s):
        return panels.at[slot, at_rows(s), :]

    def first_copy(s):
        return copy(
            piece(PANEL, s), piece(first_slot, s), a_send.at[s], panel_recv.at[first_slot, s], c, first_to
        )

    def second_copy(s):
        return copy(
            piece(PANEL, s), piece(second_slot, s), b_send.at[s], panel_recv.at[second_slot, s], c, second_to
        )

    def passed_copy(s):
        return copy(piece(1, s), piece(1, s), c_send.at[s], panel_recv.at[1, s], c, block(1))

    def panel_arrived(slot, s):
        return copy(
            piece(slot, s), piece(slot, s), panel_recv.at[slot, s], panel_recv.at[slot, s], c, d
        )

    for j in range(8):
        s = peer(j)
        if j > 0:
            copy(
                piece(PANEL, s), piece(PANEL, s), out_recv.at[s], out_recv.at[s], c, d
            ).wait_recv()
        second_copy(s).start()
        first_copy(s).start()

    def tile(left, right, slot):
        product = lax.dot_general(
            panels[left], panels[right], (((1,), (1,)), ((), ())),
            preferred_element_type=jnp.float32,
        )
        tiles[slot] = product[:, :CZ]
        tiles[slot + 1] = product[:, CZ:]

    def tile_copy(slot):
        to = slot if slot < 8 else slot - 2
        where = d if slot < 8 else block(-1)
        return copy(tiles.at[slot], sums.at[c], tile_send.at[slot], tile_recv.at[c], to, where)

    def send_tile(slot):
        for q in (slot, slot + 1):
            if q < 8:

                @pl.when(c != q)
                def _(q=q):
                    tile_copy(q).start()

                @pl.when(c == q)
                def _(q=q):
                    sums[c] = tiles[q]

            else:
                tile_copy(q).start()

    def wait_tile(slot):
        for q in (slot, slot + 1):
            if q < 8:

                @pl.when(c != q)
                def _(q=q):
                    tile_copy(q).wait_send()

            else:
                tile_copy(q).wait_send()

    tile(PANEL, PANEL, 0)
    send_tile(0)

    @pl.when(even)
    def _():
        for j in range(8):
            s = peer(j)
            panel_arrived(1, s).wait_recv()
            passed_copy(s).start()
        for s in range(8):
            panel_arrived(0, s).wait_recv()
        tile(PANEL, 0, 2)
        send_tile(2)
        tile(PANEL, 1, 4)
        send_tile(4)

    @pl.when(odd == 1)
    def _():
        for s in range(8):
            panel_arrived(0, s).wait_recv()
        tile(0, PANEL, 4)
        send_tile(4)
        for s in range(8):
            panel_arrived(1, s).wait_recv()
        tile(0, 1, 6)
        send_tile(6)
        tile(PANEL, 1, 2)
        send_tile(2)
        for s in range(8):
            panel_arrived(2, s).wait_recv()
        tile(2, PANEL, 8)
        send_tile(8)

    def sum_arrived(s):
        arrived(sums, tile_recv, s).wait_recv()

    for j in range(1, 8):
        sum_arrived(peer(j))

    @pl.when(jnp.logical_and(even, c >= 6))
    def _():
        sum_arrived(c)

    total = sums[0]
    for s in range(1, 8):
        total = total + sums[s]
    total = total * scale

    last = copy(last_out, last_in, last_send, last_recv, c, block(-2))

    @pl.when(mine)
    def _():
        out[...] = total

    @pl.when(jnp.logical_not(mine))
    def _():
        last_out[...] = total
        last.start()

    for j in range(1, 8):
        coef_copy(j).wait_send()
        in_copy(j).wait_send()
        out_copy(j).wait_send()
    for s in range(8):
        first_copy(s).wait_send()
        second_copy(s).wait_send()
    wait_tile(0)
    wait_tile(2)
    wait_tile(4)

    @pl.when(even)
    def _():
        for s in range(8):
            passed_copy(s).wait_send()

    @pl.when(odd == 1)
    def _():
        wait_tile(6)
        wait_tile(8)

    @pl.when(jnp.logical_not(mine))
    def _():
        last.wait()
        out[...] = last_in[...]


def body(sensitivity, weights, coef_x, coef_y, coef_z):
    rows, cells = sensitivity.shape
    part = rows // 8
    scale = float(cells * lax.axis_size("cells")) ** (-0.5)
    vmem = pl.BlockSpec(memory_space=pltpu.VMEM)
    dma = pltpu.SemaphoreType.DMA
    return pl.pallas_call(
        functools.partial(kernel, scale),
        out_shape=jax.ShapeDtypeStruct((rows, rows // 2), jnp.float32),
        in_specs=[pl.BlockSpec(memory_space=pl.ANY)] * 5,
        out_specs=vmem,
        scratch_shapes=[
            pltpu.VMEM((2, CZ), jnp.float32),
            pltpu.VMEM((8, 24, CZ), jnp.float32),
            pltpu.VMEM((8, 24, CZ), jnp.float32),
            pltpu.VMEM((8, part, cells), jnp.bfloat16),
            pltpu.VMEM((8, part, cells), jnp.float32),
            pltpu.VMEM((8, part, cells), jnp.bfloat16),
            pltpu.VMEM((4, rows, cells), jnp.bfloat16),
            pltpu.VMEM((10, rows, CZ), jnp.float32),
            pltpu.VMEM((8, rows, CZ), jnp.float32),
            pltpu.VMEM((rows, CZ), jnp.float32),
            pltpu.VMEM((rows, CZ), jnp.float32),
            dma((7,)), dma((8,)), dma((7,)), dma((8,)), dma((5,)), dma((7,)), dma((8,)),
            dma((8,)), dma((8,)), dma((8,)), dma((3, 8)), dma((10,)), dma((8,)), dma, dma,
        ],
        compiler_params=pltpu.CompilerParams(
            collective_id=0, has_side_effects=True, vmem_limit_bytes=60 * 1024 * 1024
        ),
        name="gram_band",
    )(
        sensitivity,
        weights.reshape(2, CZ),
        coef_x.reshape(8, CZ),
        coef_y.reshape(8, CZ),
        coef_z.reshape(8, CZ),
    )


def solution(mesh):
    return jax.shard_map(
        body,
        mesh=mesh,
        in_specs=(P("dp", "cells"), P("dp"), P("cells"), P("cells"), P("cells")),
        out_specs=P("dp", "cells"),
        check_vma=False,
    )
```

```python
import functools

import jax
import jax.numpy as jnp
from jax import lax
from jax.experimental import pallas as pl
from jax.experimental.pallas import tpu as pltpu
from jax.sharding import PartitionSpec as P

CY = 4
CZ = 128
GROUP = 16
COLUMN = 16
MESH = pl.DeviceIdType.MESH
PANEL = 3


def smoothing_pass(load, coef, store):
    def step(part, carry):
        current, entering = carry
        for half in range(2):
            if half == 0:
                above = [load(part, CY + y) for y in range(CY)]
            else:
                upper = jnp.minimum(part + 1, 7)
                above = [load(upper, y) for y in range(CY)]
            flux_x = []
            below_y = None
            for y in range(CY):
                row = half * CY + y
                here = current[y]
                flux = coef[part, pl.ds(row, 1), :] * (above[y] - here)
                change = flux - entering[y]
                flux_x.append(flux)
                if y < CY - 1:
                    flux_y = coef[part, pl.ds(8 + row, 1), :] * (current[y + 1] - here)
                    change = change + flux_y
                if y > 0:
                    change = change - below_y
                below_y = flux_y
                flux_z = coef[part, pl.ds(16 + row, 1), :] * (pltpu.roll(here, CZ - 1, 1) - here)
                change = change + (flux_z - pltpu.roll(flux_z, 1, 1))
                store(part, row, here + change)
            current, entering = tuple(above), tuple(flux_x)
        return current, entering

    first = tuple(load(0, y) for y in range(CY))
    zero = tuple(jnp.zeros((GROUP, CZ), jnp.float32) for _ in range(CY))
    lax.fori_loop(0, 8, step, (first, zero))


def kernel(
    scale, sens, weights_hbm, coef_x, coef_y, coef_z, out,
    weights, gathered, coef, slab_in, field, slab_out, panels, tiles, sums, last_out, last_in, relay,
    coef_send, coef_recv, in_send, in_recv, own_sem, out_send, out_recv,
    a_send, b_send, c_send, panel_recv, tile_send, tile_recv, last_send, last_recv,
    relay_send, relay_recv,
):
    c = lax.axis_index("cells")
    d = lax.axis_index("dp")
    blocks = lax.axis_size("dp")
    odd = lax.rem(d, 2)
    even = odd == 0
    height = lax.rem(d, COLUMN) // 2
    bottom, top = height == 0, height == COLUMN // 2 - 1
    edge = jnp.logical_or(bottom, top)
    rows = sens.shape[0] // 8

    def block(offset):
        return lax.rem(d + offset + blocks, blocks)

    def peer(j):
        return lax.rem(c + j, 8)

    def at_rows(index):
        return pl.ds(pl.multiple_of(index * rows, rows), rows)

    mine = jnp.logical_or(c < 4, jnp.logical_and(even, c < 6))

    barrier = pltpu.get_barrier_semaphore()

    def greet(cells, dp):
        pl.semaphore_signal(barrier, inc=1, device_id=(cells, dp), device_id_type=MESH)

    for j in range(1, 8):
        greet(peer(j), d)

    @pl.when(even)
    def _():
        greet(c, block(1))
        greet(c, block(2))

        @pl.when(c >= 6)
        def _():
            for j in range(1, 8):
                greet(peer(j), block(1))

    @pl.when(odd == 1)
    def _():
        greet(c, block(-1))
        greet(c, block(-2))
        greet(c, block(-3))

        @pl.when(c >= 4)
        def _():
            greet(c, block(2))

    @pl.when(bottom)
    def _():
        greet(c, block(COLUMN - 2))

        @pl.when(odd == 1)
        def _():
            greet(c, block(-COLUMN - 1))
            greet(c, block(-COLUMN))

    @pl.when(jnp.logical_and(top, even))
    def _():
        greet(c, block(2 - COLUMN))
        greet(c, block(COLUMN))

    own = [
        pltpu.make_async_copy(source, target, own_sem.at[i])
        for i, (source, target) in enumerate(
            [
                (coef_x, gathered.at[c, pl.ds(0, 8), :]),
                (coef_y, gathered.at[c, pl.ds(8, 8), :]),
                (coef_z, gathered.at[c, pl.ds(16, 8), :]),
                (weights_hbm, weights),
                (sens.at[at_rows(c), :], slab_in.at[c]),
            ]
        )
    ]
    for one in own:
        one.start()

    to_odd = 11 - (c >= 6).astype(jnp.int32) + (c >= 4).astype(jnp.int32)
    to_relay = edge.astype(jnp.int32) * (2 - odd)
    pl.semaphore_wait(barrier, jnp.where(even, 10, to_odd) + to_relay)

    def copy(source, target, send, recv, cells, dp):
        return pltpu.make_async_remote_copy(
            src_ref=source, dst_ref=target, send_sem=send, recv_sem=recv,
            device_id=(cells, dp), device_id_type=MESH,
        )

    def coef_copy(j):
        return copy(
            gathered.at[c], gathered.at[c], coef_send.at[j - 1], coef_recv.at[c], peer(j), d
        )

    def in_copy(j):
        to = peer(j)
        return copy(sens.at[at_rows(to), :], slab_in.at[c], in_send.at[j - 1], in_recv.at[c], to, d)

    for one in own[:3]:
        one.wait()
    for j in range(1, 8):
        coef_copy(j).start()
    for j in range(1, 8):
        in_copy(j).start()

    own[3].wait()
    lane = lax.broadcasted_iota(jnp.int32, (rows, CZ), 1)
    line = lax.broadcasted_iota(jnp.int32, (rows, CZ), 0)
    weight_row = jnp.where(c < 4, weights[0:1, :], weights[1:2, :])
    chosen = lane == line + lax.rem(c, 4) * rows
    weight = jnp.sum(jnp.where(chosen, weight_row, 0.0), axis=1, keepdims=True)

    def arrived(buffer, sem, s):
        return copy(buffer.at[s], buffer.at[s], sem.at[s], sem.at[s], c, d)

    for j in range(1, 8):
        arrived(gathered, coef_recv, peer(j)).wait_recv()
    inner = lax.broadcasted_iota(jnp.int32, (8, CZ), 1) < CZ - 1
    for s in range(8):
        if s < 7:
            coef[s, 0:8, :] = gathered[s, 0:8, :]
        else:
            coef[s, 0:4, :] = gathered[s, 0:4, :]
            coef[s, 4:8, :] = jnp.zeros((4, CZ), jnp.float32)
        coef[s, 8:16, :] = gathered[s, 8:16, :]
        coef[s, 16:24, :] = jnp.where(inner, gathered[s, 16:24, :], 0.0)
    own[4].wait()
    for j in range(1, 8):
        arrived(slab_in, in_recv, peer(j)).wait_recv()

    for group in range(rows // GROUP):
        part_rows = pl.ds(group * GROUP, GROUP)
        scaled = weight[group * GROUP : (group + 1) * GROUP]

        def load_in(part, tile, part_rows=part_rows):
            return slab_in[part, part_rows, pl.ds(tile * CZ, CZ)].astype(jnp.float32)

        def store_field(part, tile, value, part_rows=part_rows):
            field[part, part_rows, pl.ds(tile * CZ, CZ)] = value

        def load_field(part, tile, part_rows=part_rows):
            return field[part, part_rows, pl.ds(tile * CZ, CZ)]

        def store_out(part, tile, value, part_rows=part_rows, scaled=scaled):
            slab_out[part, part_rows, pl.ds(tile * CZ, CZ)] = (scaled * value).astype(jnp.bfloat16)

        smoothing_pass(load_in, coef, store_field)
        smoothing_pass(load_field, coef, store_out)

    def out_copy(j):
        to = peer(j)
        return copy(
            slab_out.at[to], panels.at[PANEL, at_rows(c), :], out_send.at[j - 1], out_recv.at[c], to, d
        )

    for j in range(1, 8):
        out_copy(j).start()
    panels[PANEL, at_rows(c), :] = slab_out[c]

    first_to = jnp.where(even, block(-2), block(-1))
    first_slot = jnp.where(even, 1, 0)
    second_to = jnp.where(even, block(3), block(2))
    second_slot = jnp.where(even, 2, 0)

    def piece(slot, s):
        return panels.at[slot, at_rows(s), :]

    def first_copy(s):
        return copy(
            piece(PANEL, s), piece(first_slot, s), a_send.at[s], panel_recv.at[first_slot, s], c, first_to
        )

    def second_copy(s):
        return copy(
            piece(PANEL, s), piece(second_slot, s), b_send.at[s], panel_recv.at[second_slot, s], c, second_to
        )

    relay_to = jnp.where(bottom, block(COLUMN - 2), block(2 - COLUMN))
    relayed_to = jnp.where(bottom, block(COLUMN + 1 - odd), block(-COLUMN))
    relayed_slot = jnp.where(bottom, second_slot, 1)

    def to_relay_copy(s, send):
        return copy(
            piece(PANEL, s), relay.at[s // 2], send.at[s], relay_recv.at[s // 2], c, relay_to
        )

    def relayed_copy(i):
        s = 2 * i + 1
        return copy(
            relay.at[i], piece(relayed_slot, s), relay_send.at[i], panel_recv.at[relayed_slot, s], c, relayed_to
        )

    relays = jnp.logical_or(bottom, jnp.logical_and(top, even))

    def passed_copy(s):
        return copy(piece(1, s), piece(1, s), c_send.at[s], panel_recv.at[1, s], c, block(1))

    def panel_arrived(slot, s):
        return copy(
            piece(slot, s), piece(slot, s), panel_recv.at[slot, s], panel_recv.at[slot, s], c, d
        )

    for j in range(8):
        s = peer(j)
        if j > 0:
            copy(
                piece(PANEL, s), piece(PANEL, s), out_recv.at[s], out_recv.at[s], c, d
            ).wait_recv()
        indirect = lax.rem(s, 2) == 1
        second_indirect = jnp.logical_and(indirect, top)
        first_indirect = jnp.logical_and(indirect, jnp.logical_and(bottom, even))

        @pl.when(second_indirect)
        def _(s=s):
            to_relay_copy(s, b_send).start()

        @pl.when(jnp.logical_not(second_indirect))
        def _(s=s):
            second_copy(s).start()

        @pl.when(first_indirect)
        def _(s=s):
            to_relay_copy(s, a_send).start()

        @pl.when(jnp.logical_not(first_indirect))
        def _(s=s):
            first_copy(s).start()

    def tile(left, right, slot):
        product = lax.dot_general(
            panels[left], panels[right], (((1,), (1,)), ((), ())),
            preferred_element_type=jnp.float32,
        )
        tiles[slot] = product[:, :CZ]
        tiles[slot + 1] = product[:, CZ:]

    def tile_copy(slot):
        to = slot if slot < 8 else slot - 2
        where = d if slot < 8 else block(-1)
        return copy(tiles.at[slot], sums.at[c], tile_send.at[slot], tile_recv.at[c], to, where)

    def send_tile(slot):
        for q in (slot, slot + 1):
            if q < 8:

                @pl.when(c != q)
                def _(q=q):
                    tile_copy(q).start()

                @pl.when(c == q)
                def _(q=q):
                    sums[c] = tiles[q]

            else:
                tile_copy(q).start()

    def wait_tile(slot):
        for q in (slot, slot + 1):
            if q < 8:

                @pl.when(c != q)
                def _(q=q):
                    tile_copy(q).wait_send()

            else:
                tile_copy(q).wait_send()

    tile(PANEL, PANEL, 0)
    send_tile(0)

    @pl.when(relays)
    def _():
        for i in range(4):
            arrived(relay, relay_recv, i).wait_recv()
            relayed_copy(i).start()

    @pl.when(even)
    def _():
        for j in range(8):
            s = peer(j)
            panel_arrived(1, s).wait_recv()
            passed_copy(s).start()
        for s in range(8):
            panel_arrived(0, s).wait_recv()
        tile(PANEL, 0, 2)
        send_tile(2)
        tile(PANEL, 1, 4)
        send_tile(4)

    @pl.when(odd == 1)
    def _():
        for s in range(8):
            panel_arrived(0, s).wait_recv()
        tile(0, PANEL, 4)
        send_tile(4)
        for s in range(8):
            panel_arrived(1, s).wait_recv()
        tile(0, 1, 6)
        send_tile(6)
        tile(PANEL, 1, 2)
        send_tile(2)
        for s in range(8):
            panel_arrived(2, s).wait_recv()
        tile(2, PANEL, 8)
        send_tile(8)

    def sum_arrived(s):
        arrived(sums, tile_recv, s).wait_recv()

    for j in range(1, 8):
        sum_arrived(peer(j))

    @pl.when(jnp.logical_and(even, c >= 6))
    def _():
        sum_arrived(c)

    total = sums[0]
    for s in range(1, 8):
        total = total + sums[s]
    total = total * scale

    last = copy(last_out, last_in, last_send, last_recv, c, block(-2))

    @pl.when(mine)
    def _():
        out[...] = total

    @pl.when(jnp.logical_not(mine))
    def _():
        last_out[...] = total
        last.start()

    for j in range(1, 8):
        coef_copy(j).wait_send()
        in_copy(j).wait_send()
        out_copy(j).wait_send()
    for s in range(8):
        first_copy(s).wait_send()
        second_copy(s).wait_send()
    wait_tile(0)
    wait_tile(2)
    wait_tile(4)

    @pl.when(relays)
    def _():
        for i in range(4):
            relayed_copy(i).wait_send()

    @pl.when(even)
    def _():
        for s in range(8):
            passed_copy(s).wait_send()

    @pl.when(odd == 1)
    def _():
        wait_tile(6)
        wait_tile(8)

    @pl.when(jnp.logical_not(mine))
    def _():
        last.wait()
        out[...] = last_in[...]


def body(sensitivity, weights, coef_x, coef_y, coef_z):
    rows, cells = sensitivity.shape
    part = rows // 8
    scale = float(cells * lax.axis_size("cells")) ** (-0.5)
    vmem = pl.BlockSpec(memory_space=pltpu.VMEM)
    dma = pltpu.SemaphoreType.DMA
    return pl.pallas_call(
        functools.partial(kernel, scale),
        out_shape=jax.ShapeDtypeStruct((rows, rows // 2), jnp.float32),
        in_specs=[pl.BlockSpec(memory_space=pl.ANY)] * 5,
        out_specs=vmem,
        scratch_shapes=[
            pltpu.VMEM((2, CZ), jnp.float32),
            pltpu.VMEM((8, 24, CZ), jnp.float32),
            pltpu.VMEM((8, 24, CZ), jnp.float32),
            pltpu.VMEM((8, part, cells), jnp.bfloat16),
            pltpu.VMEM((8, part, cells), jnp.float32),
            pltpu.VMEM((8, part, cells), jnp.bfloat16),
            pltpu.VMEM((4, rows, cells), jnp.bfloat16),
            pltpu.VMEM((10, rows, CZ), jnp.float32),
            pltpu.VMEM((8, rows, CZ), jnp.float32),
            pltpu.VMEM((rows, CZ), jnp.float32),
            pltpu.VMEM((rows, CZ), jnp.float32),
            pltpu.VMEM((4, part, cells), jnp.bfloat16),
            dma((7,)), dma((8,)), dma((7,)), dma((8,)), dma((5,)), dma((7,)), dma((8,)),
            dma((8,)), dma((8,)), dma((8,)), dma((3, 8)), dma((10,)), dma((8,)), dma, dma,
            dma((4,)), dma((4,)),
        ],
        compiler_params=pltpu.CompilerParams(
            collective_id=0, has_side_effects=True, vmem_limit_bytes=60 * 1024 * 1024
        ),
        name="gram_band",
    )(
        sensitivity,
        weights.reshape(2, CZ),
        coef_x.reshape(8, CZ),
        coef_y.reshape(8, CZ),
        coef_z.reshape(8, CZ),
    )


def solution(mesh):
    return jax.shard_map(
        body,
        mesh=mesh,
        in_specs=(P("dp", "cells"), P("dp"), P("cells"), P("cells"), P("cells")),
        out_specs=P("dp", "cells"),
        check_vma=False,
    )
```

```python
import functools

import jax
import jax.numpy as jnp
from jax import lax
from jax.experimental import pallas as pl
from jax.experimental.pallas import tpu as pltpu
from jax.sharding import PartitionSpec as P

CY = 4
CZ = 128
GROUP = 16
COLUMN = 16
MESH = pl.DeviceIdType.MESH
PANEL = 3


def smoothing_pass(load, coef, store):
    def step(part, carry):
        current, entering = carry
        for half in range(2):
            if half == 0:
                above = [load(part, CY + y) for y in range(CY)]
            else:
                upper = jnp.minimum(part + 1, 7)
                above = [load(upper, y) for y in range(CY)]
            flux_x = []
            below_y = None
            for y in range(CY):
                row = half * CY + y
                here = current[y]
                flux = coef[part, pl.ds(row, 1), :] * (above[y] - here)
                change = flux - entering[y]
                flux_x.append(flux)
                if y < CY - 1:
                    flux_y = coef[part, pl.ds(8 + row, 1), :] * (current[y + 1] - here)
                    change = change + flux_y
                if y > 0:
                    change = change - below_y
                below_y = flux_y
                flux_z = coef[part, pl.ds(16 + row, 1), :] * (pltpu.roll(here, CZ - 1, 1) - here)
                change = change + (flux_z - pltpu.roll(flux_z, 1, 1))
                store(part, row, here + change)
            current, entering = tuple(above), tuple(flux_x)
        return current, entering

    first = tuple(load(0, y) for y in range(CY))
    zero = tuple(jnp.zeros((GROUP, CZ), jnp.float32) for _ in range(CY))
    lax.fori_loop(0, 8, step, (first, zero), unroll=4)


def kernel(
    scale, sens, weights_hbm, coef_x, coef_y, coef_z, out,
    weights, gathered, coef, slab_in, field, slab_out, panels, tiles, sums, late_sums, last_out, last_in, relay,
    coef_send, coef_recv, in_send, in_recv, own_sem, out_send, out_recv,
    a_send, b_send, c_send, panel_recv, tile_send, tile_recv, last_send, last_recv,
    relay_send, relay_recv, late, edge_send, late_recv,
):
    c = lax.axis_index("cells")
    d = lax.axis_index("dp")
    blocks = lax.axis_size("dp")
    odd = lax.rem(d, 2)
    even = odd == 0
    height = lax.rem(d, COLUMN) // 2
    bottom, top = height == 0, height == COLUMN // 2 - 1
    inner_bottom, inner_top = jnp.logical_not(bottom), jnp.logical_not(top)
    first_column, last_column = d < COLUMN, d >= blocks - COLUMN
    rows = sens.shape[0] // 8

    def block(offset):
        return lax.rem(d + offset + blocks, blocks)

    def peer(j):
        return lax.rem(c + j, 8)

    def at_rows(index):
        return pl.ds(pl.multiple_of(index * rows, rows), rows)

    mine = jnp.logical_or(c < 4, even)

    barrier = pltpu.get_barrier_semaphore()

    def greet(cells, dp):
        pl.semaphore_signal(barrier, inc=1, device_id=(cells, dp), device_id_type=MESH)

    def when(*conditions):
        return pl.when(functools.reduce(jnp.logical_and, conditions))

    for j in range(1, 8):
        greet(peer(j), d)
    greet(c, d + 1 - 2 * odd)

    @when(odd == 1, c >= 4, c < 6, top)
    def _():
        for j in range(1, 8):
            greet(peer(j), block(-1))

    @when(inner_top)
    def _():
        greet(c, block(2))

        @pl.when(even)
        def _():
            greet(c, block(3))

    @when(bottom)
    def _():
        greet(c, block(COLUMN - 2))
        greet(c, block(-2))

        @pl.when(odd == 1)
        def _():
            greet(c, block(-3))

    @when(top, even, jnp.logical_not(last_column))
    def _():
        greet(c, block(COLUMN))
        greet(c, block(COLUMN + 1))

    @when(top, first_column)
    def _():
        greet(c, block(-COLUMN - odd))

    own = [
        pltpu.make_async_copy(source, target, own_sem.at[i])
        for i, (source, target) in enumerate(
            [
                (coef_x, gathered.at[c, pl.ds(0, 8), :]),
                (coef_y, gathered.at[c, pl.ds(8, 8), :]),
                (coef_z, gathered.at[c, pl.ds(16, 8), :]),
                (weights_hbm, weights),
                (sens.at[at_rows(c), :], slab_in.at[c]),
            ]
        )
    ]
    for one in own:
        one.start()

    def count(*conditions):
        return functools.reduce(jnp.logical_and, conditions).astype(jnp.int32)

    present = jnp.int32(8)
    present += count(even, top) * 2 - count(even, top, c >= 4, c < 6)
    present += count(inner_bottom) * (1 + odd)
    present += count(top) * (3 - odd) + count(top, jnp.logical_not(first_column))
    present += count(top, even, last_column) * 2
    pl.semaphore_wait(barrier, present)

    def answer(dp):
        pl.semaphore_signal(late, inc=1, device_id=(c, dp), device_id_type=MESH)

    @when(odd == 1, inner_bottom)
    def _():
        answer(block(-2))

    @when(top)
    def _():
        answer(block(2 - COLUMN))

        @pl.when(even)
        def _():
            answer(block(2))
            answer(block(3))

        @when(odd == 1, c >= 6)
        def _():
            answer(block(2))

    @when(top, even, last_column)
    def _():
        answer(block(COLUMN))
        answer(block(COLUMN + 1))

    def copy(source, target, send, recv, cells, dp):
        return pltpu.make_async_remote_copy(
            src_ref=source, dst_ref=target, send_sem=send, recv_sem=recv,
            device_id=(cells, dp), device_id_type=MESH,
        )

    def coef_copy(j):
        return copy(
            gathered.at[c], gathered.at[c], coef_send.at[j - 1], coef_recv.at[c], peer(j), d
        )

    def in_copy(j):
        to = peer(j)
        return copy(sens.at[at_rows(to), :], slab_in.at[c], in_send.at[j - 1], in_recv.at[c], to, d)

    for one in own[:3]:
        one.wait()
    for j in range(1, 8):
        coef_copy(j).start()
    for j in range(1, 8):
        in_copy(j).start()

    own[3].wait()
    lane = lax.broadcasted_iota(jnp.int32, (rows, CZ), 1)
    line = lax.broadcasted_iota(jnp.int32, (rows, CZ), 0)
    weight_row = jnp.where(c < 4, weights[0:1, :], weights[1:2, :])
    chosen = lane == line + lax.rem(c, 4) * rows
    weight = jnp.sum(jnp.where(chosen, weight_row, 0.0), axis=1, keepdims=True)

    def arrived(buffer, sem, s):
        return copy(buffer.at[s], buffer.at[s], sem.at[s], sem.at[s], c, d)

    for j in range(1, 8):
        arrived(gathered, coef_recv, peer(j)).wait_recv()
    inner = lax.broadcasted_iota(jnp.int32, (8, CZ), 1) < CZ - 1
    for s in range(8):
        if s < 7:
            coef[s, 0:8, :] = gathered[s, 0:8, :]
        else:
            coef[s, 0:4, :] = gathered[s, 0:4, :]
            coef[s, 4:8, :] = jnp.zeros((4, CZ), jnp.float32)
        coef[s, 8:16, :] = gathered[s, 8:16, :]
        coef[s, 16:24, :] = jnp.where(inner, gathered[s, 16:24, :], 0.0)
    own[4].wait()
    for j in range(1, 8):
        arrived(slab_in, in_recv, peer(j)).wait_recv()

    for group in range(rows // GROUP):
        part_rows = pl.ds(group * GROUP, GROUP)
        scaled = weight[group * GROUP : (group + 1) * GROUP]

        def load_in(part, tile, part_rows=part_rows):
            return slab_in[part, part_rows, pl.ds(tile * CZ, CZ)].astype(jnp.float32)

        def store_field(part, tile, value, part_rows=part_rows):
            field[part, part_rows, pl.ds(tile * CZ, CZ)] = value

        def load_field(part, tile, part_rows=part_rows):
            return field[part, part_rows, pl.ds(tile * CZ, CZ)]

        def store_out(part, tile, value, part_rows=part_rows, scaled=scaled):
            slab_out[part, part_rows, pl.ds(tile * CZ, CZ)] = (scaled * value).astype(jnp.bfloat16)

        smoothing_pass(load_in, coef, store_field)
        smoothing_pass(load_field, coef, store_out)

    def out_copy(j):
        to = peer(j)
        return copy(
            slab_out.at[to], panels.at[PANEL, at_rows(c), :], out_send.at[j - 1], out_recv.at[c], to, d
        )

    for j in range(1, 8):
        out_copy(j).start()
    panels[PANEL, at_rows(c), :] = slab_out[c]

    first_to = jnp.where(even, block(-2), block(-1))
    first_slot = jnp.where(even, 1, 0)
    def piece(slot, s):
        return panels.at[slot, at_rows(s), :]

    def first_copy(s):
        return copy(
            piece(PANEL, s), piece(first_slot, s), a_send.at[s], panel_recv.at[first_slot, s], c, first_to
        )

    def second_copy(s):
        return copy(piece(PANEL, s), piece(0, s), b_send.at[s], panel_recv.at[0, s], c, block(2))

    relayed_slot = 1 + odd

    def to_relay_copy(s, send):
        return copy(
            piece(PANEL, s), relay.at[s // 2], send.at[s], relay_recv.at[s // 2], c, block(COLUMN - 2)
        )

    def relayed_copy(i):
        s = 2 * i + 1
        return copy(
            relay.at[i], piece(relayed_slot, s), relay_send.at[i], panel_recv.at[relayed_slot, s], c, block(-COLUMN - odd)
        )

    def third_copy(s):
        return copy(piece(PANEL, s), piece(2, s), edge_send.at[s], panel_recv.at[2, s], c, block(-3))

    @when(top)
    def _():
        for i in range(4):
            arrived(relay, relay_recv, i).wait_recv()
            relayed_copy(i).start()

    awaited = count(odd == 1, inner_top) + count(bottom) * 2
    awaited += count(bottom, odd == 1, c >= 6) + count(top, first_column)

    @pl.when(awaited > 0)
    def _():
        pl.semaphore_wait(late, awaited)

    def passed_copy(s):
        return copy(piece(1, s), piece(1, s), c_send.at[s], panel_recv.at[1, s], c, block(1))

    def panel_arrived(slot, s):
        return copy(
            piece(slot, s), piece(slot, s), panel_recv.at[slot, s], panel_recv.at[slot, s], c, d
        )

    for j in range(8):
        s = peer(j)
        if j > 0:
            copy(
                piece(PANEL, s), piece(PANEL, s), out_recv.at[s], out_recv.at[s], c, d
            ).wait_recv()
        indirect = lax.rem(s, 2) == 1

        @pl.when(odd == 1)
        def _(s=s):
            second_copy(s).start()

        @when(bottom, indirect, even)
        def _(s=s):
            to_relay_copy(s, a_send).start()

        @pl.when(jnp.logical_not(jnp.logical_and(bottom, jnp.logical_and(indirect, even))))
        def _(s=s):
            first_copy(s).start()

    def tile(left, right, slot):
        product = lax.dot_general(
            panels[left], panels[right], (((1,), (1,)), ((), ())),
            preferred_element_type=jnp.float32,
        )
        tiles[slot] = product[:, :CZ]
        tiles[slot + 1] = product[:, CZ:]

    def tile_copy(slot):
        if slot < 8:
            return copy(tiles.at[slot], sums.at[c], tile_send.at[slot], tile_recv.at[c], slot, d)
        return copy(
            tiles.at[slot], late_sums.at[c], tile_send.at[slot], late_recv.at[c], slot - 4, block(1)
        )

    def send_tile(slot):
        for q in (slot, slot + 1):
            if q < 8:

                @pl.when(c != q)
                def _(q=q):
                    tile_copy(q).start()

                @pl.when(c == q)
                def _(q=q):
                    sums[c] = tiles[q]

            else:
                tile_copy(q).start()

    def wait_tile(slot):
        for q in (slot, slot + 1):
            if q < 8:

                @pl.when(c != q)
                def _(q=q):
                    tile_copy(q).wait_send()

            else:
                tile_copy(q).wait_send()

    tile(PANEL, PANEL, 0)
    send_tile(0)

    @pl.when(even)
    def _():
        for s in range(8):
            panel_arrived(0, s).wait_recv()
        tile(PANEL, 0, 2)
        send_tile(2)
        for j in range(8):
            s = peer(j)
            panel_arrived(1, s).wait_recv()
            passed_copy(s).start()
        tile(PANEL, 1, 4)
        send_tile(4)
        for s in range(8):
            panel_arrived(2, s).wait_recv()
        tile(PANEL, 2, 6)
        send_tile(6)

        @pl.when(top)
        def _():
            tile(0, 2, 8)
            send_tile(8)

    @pl.when(odd == 1)
    def _():
        for j in range(8):
            s = peer(j)
            indirect = jnp.logical_and(lax.rem(s, 2) == 1, bottom)

            @pl.when(indirect)
            def _(s=s):
                to_relay_copy(s, edge_send).start()

            @pl.when(jnp.logical_not(indirect))
            def _(s=s):
                third_copy(s).start()

        @pl.when(inner_bottom)
        def _():
            for s in range(8):
                panel_arrived(0, s).wait_recv()
            tile(0, PANEL, 4)
            send_tile(4)

        for s in range(8):
            panel_arrived(1, s).wait_recv()

        @pl.when(bottom)
        def _():
            tile(PANEL, 1, 2)
            send_tile(2)
            for s in range(8):
                panel_arrived(0, s).wait_recv()

        tile(0, 1, 6)
        send_tile(6)

        @pl.when(inner_bottom)
        def _():
            tile(PANEL, 1, 2)
            send_tile(2)

    guest = jnp.logical_not(mine)

    def total(landing):
        value = landing[0]
        for s in range(1, 8):
            value = value + landing[s]
        return value * scale

    crossing = c >= 6
    gives = jnp.logical_and(guest, jnp.logical_or(inner_bottom, crossing))
    takes = jnp.logical_and(guest, jnp.logical_or(inner_top, crossing))
    last = copy(last_out, last_in, last_send, last_recv, c, block(-2))

    @pl.when(mine)
    def _():
        for j in range(1, 8):
            arrived(sums, tile_recv, peer(j)).wait_recv()
        out[...] = total(sums)

    @pl.when(gives)
    def _():
        for j in range(1, 8):
            arrived(sums, tile_recv, peer(j)).wait_recv()

        last_out[...] = total(sums)
        last.start()

    @when(guest, jnp.logical_not(takes))
    def _():
        for j in range(1, 8):
            arrived(late_sums, late_recv, peer(j)).wait_recv()

        arrived(late_sums, late_recv, c).wait_recv()
        out[...] = total(late_sums)

    @pl.when(takes)
    def _():
        last.wait_recv()
        out[...] = last_in[...]

    for j in range(1, 8):
        coef_copy(j).wait_send()
        in_copy(j).wait_send()
        out_copy(j).wait_send()
    for s in range(8):
        first_copy(s).wait_send()
    wait_tile(0)
    wait_tile(2)

    @when(top)
    def _():
        for i in range(4):
            relayed_copy(i).wait_send()

    @pl.when(even)
    def _():
        for s in range(8):
            passed_copy(s).wait_send()
        wait_tile(4)

        @pl.when(top)
        def _():
            wait_tile(8)

    @pl.when(odd == 1)
    def _():
        for s in range(8):
            second_copy(s).wait_send()
            third_copy(s).wait_send()

        @pl.when(inner_bottom)
        def _():
            wait_tile(4)

    wait_tile(6)

    @pl.when(gives)
    def _():
        last.wait_send()


def body(sensitivity, weights, coef_x, coef_y, coef_z):
    rows, cells = sensitivity.shape
    part = rows // 8
    scale = float(cells * lax.axis_size("cells")) ** (-0.5)
    vmem = pl.BlockSpec(memory_space=pltpu.VMEM)
    dma = pltpu.SemaphoreType.DMA
    return pl.pallas_call(
        functools.partial(kernel, scale),
        out_shape=jax.ShapeDtypeStruct((rows, rows // 2), jnp.float32),
        in_specs=[pl.BlockSpec(memory_space=pl.ANY)] * 5,
        out_specs=vmem,
        scratch_shapes=[
            pltpu.VMEM((2, CZ), jnp.float32),
            pltpu.VMEM((8, 24, CZ), jnp.float32),
            pltpu.VMEM((8, 24, CZ), jnp.float32),
            pltpu.VMEM((8, part, cells), jnp.bfloat16),
            pltpu.VMEM((8, part, cells), jnp.float32),
            pltpu.VMEM((8, part, cells), jnp.bfloat16),
            pltpu.VMEM((4, rows, cells), jnp.bfloat16),
            pltpu.VMEM((10, rows, CZ), jnp.float32),
            pltpu.VMEM((8, rows, CZ), jnp.float32),
            pltpu.VMEM((8, rows, CZ), jnp.float32),
            pltpu.VMEM((rows, CZ), jnp.float32),
            pltpu.VMEM((rows, CZ), jnp.float32),
            pltpu.VMEM((4, part, cells), jnp.bfloat16),
            dma((7,)), dma((8,)), dma((7,)), dma((8,)), dma((5,)), dma((7,)), dma((8,)),
            dma((8,)), dma((8,)), dma((8,)), dma((3, 8)), dma((10,)), dma((8,)), dma, dma,
            dma((4,)), dma((4,)), pltpu.SemaphoreType.REGULAR, dma((8,)), dma((8,)),
        ],
        compiler_params=pltpu.CompilerParams(
            collective_id=0, has_side_effects=True, vmem_limit_bytes=60 * 1024 * 1024
        ),
        name="gram_band",
    )(
        sensitivity,
        weights.reshape(2, CZ),
        coef_x.reshape(8, CZ),
        coef_y.reshape(8, CZ),
        coef_z.reshape(8, CZ),
    )


def solution(mesh):
    return jax.shard_map(
        body,
        mesh=mesh,
        in_specs=(P("dp", "cells"), P("dp"), P("cells"), P("cells"), P("cells")),
        out_specs=P("dp", "cells"),
        check_vma=False,
    )
```

```python
import functools

import jax
import jax.numpy as jnp
from jax import lax
from jax.experimental import pallas as pl
from jax.experimental.pallas import tpu as pltpu
from jax.sharding import PartitionSpec as P

CY = 4
CZ = 128
GROUP = 16
GROUPS = 2
CHUNKS = 4
COLUMN = 16
MESH = pl.DeviceIdType.MESH
PANEL = 3


def smoothing_pass(load, coef, store):
    def step(part, carry):
        current, entering = carry
        for half in range(2):
            if half == 0:
                above = [load(part, CY + y) for y in range(CY)]
            else:
                upper = jnp.minimum(part + 1, 7)
                above = [load(upper, y) for y in range(CY)]
            flux_x = []
            below_y = None
            for y in range(CY):
                row = half * CY + y
                here = current[y]
                flux = coef[part, pl.ds(row, 1), :] * (above[y] - here)
                change = flux - entering[y]
                flux_x.append(flux)
                if y < CY - 1:
                    flux_y = coef[part, pl.ds(8 + row, 1), :] * (current[y + 1] - here)
                    change = change + flux_y
                if y > 0:
                    change = change - below_y
                below_y = flux_y
                flux_z = coef[part, pl.ds(16 + row, 1), :] * (pltpu.roll(here, CZ - 1, 1) - here)
                change = change + (flux_z - pltpu.roll(flux_z, 1, 1))
                store(part, row, here + change)
            current, entering = tuple(above), tuple(flux_x)
        return current, entering

    first = tuple(load(0, y) for y in range(CY))
    zero = tuple(jnp.zeros((GROUP, CZ), jnp.float32) for _ in range(CY))
    lax.fori_loop(0, 8, step, (first, zero), unroll=4)


def kernel(
    scale, sens, weights_hbm, coef_x, coef_y, coef_z, out,
    weights, gathered, coef, slab_in, field, slab_out, panels, tiles, sums, reduced, landing, relay,
    coef_send, coef_recv, in_send, in_recv, own_sem, out_send, out_recv,
    a_send, b_send, c_send, panel_recv, tile_send, tile_recv, last_send, last_recv,
    relay_send, relay_recv, late, edge_send,
):
    c = lax.axis_index("cells")
    d = lax.axis_index("dp")
    blocks = lax.axis_size("dp")
    odd = lax.rem(d, 2)
    even = odd == 0
    height = lax.rem(d, COLUMN) // 2
    bottom, top = height == 0, height == COLUMN // 2 - 1
    inner_bottom, inner_top = jnp.logical_not(bottom), jnp.logical_not(top)
    first_column, last_column = d < COLUMN, d >= blocks - COLUMN
    rows = sens.shape[0] // 8

    def block(offset):
        return lax.rem(d + offset + blocks, blocks)

    def peer(j):
        return lax.rem(c + j, 8)

    def at_rows(index):
        return pl.ds(pl.multiple_of(index * rows, rows), rows)


    def rows_of(group, index):
        start = group * (8 * GROUP) + index * GROUP
        return pl.ds(pl.multiple_of(start, GROUP), GROUP)

    def slab_rows(group):
        return pl.ds(group * GROUP, GROUP)

    barrier = pltpu.get_barrier_semaphore()

    def greet(cells, dp):
        pl.semaphore_signal(barrier, inc=1, device_id=(cells, dp), device_id_type=MESH)

    def when(*conditions):
        return pl.when(functools.reduce(jnp.logical_and, conditions))

    for j in range(1, 8):
        greet(peer(j), d)
    greet(c, d + 1 - 2 * odd)

    @when(odd == 1, c >= 4, c < 6, top)
    def _():
        for j in range(1, 8):
            greet(peer(j), block(-1))

    @when(inner_top)
    def _():
        greet(c, block(2))

        @pl.when(even)
        def _():
            greet(c, block(3))

    @when(inner_top, odd == 1, c >= 4)
    def _():
        for j in range(1, 8):
            greet(peer(j), block(2))

    @when(bottom)
    def _():
        greet(c, block(COLUMN - 2))
        greet(c, block(-2))

        @pl.when(odd == 1)
        def _():
            greet(c, block(-3))
            for q in (6, 7):

                @pl.when(c != q)
                def _(q=q):
                    greet(q, block(-2))

        @when(odd == 1, jnp.logical_not(last_column))
        def _():
            greet(c, block(COLUMN))

        @when(odd == 1, first_column)
        def _():
            greet(c, block(-COLUMN))

    @when(top, even, jnp.logical_not(last_column))
    def _():
        greet(c, block(COLUMN))
        greet(c, block(COLUMN + 1))

    @when(top, first_column)
    def _():
        greet(c, block(-COLUMN - odd))

    own = [
        pltpu.make_async_copy(source, target, own_sem.at[i])
        for i, (source, target) in enumerate(
            [
                (coef_x, gathered.at[c, pl.ds(0, 8), :]),
                (coef_y, gathered.at[c, pl.ds(8, 8), :]),
                (coef_z, gathered.at[c, pl.ds(16, 8), :]),
                (weights_hbm, weights),
            ]
            + [
                (sens.at[rows_of(group, c), :], slab_in.at[c, slab_rows(group), :])
                for group in range(GROUPS)
            ]
        )
    ]
    for one in own:
        one.start()

    def count(*conditions):
        return functools.reduce(jnp.logical_and, conditions).astype(jnp.int32)

    present = 8 + count(odd == 1, inner_bottom) * 4 - count(odd == 1, inner_bottom, c >= 4)
    present += count(top, odd == 1, c >= 6) * 7
    present += count(bottom, odd == 1, jnp.logical_not(first_column))
    present += count(bottom, odd == 1, last_column)
    present += count(even, top) * 2 - count(even, top, c >= 4, c < 6)
    present += count(inner_bottom) * (1 + odd)
    present += count(top) * (3 - odd) + count(top, jnp.logical_not(first_column))
    present += count(top, even, last_column) * 2
    pl.semaphore_wait(barrier, present)

    def answer(dp, cells=c):
        pl.semaphore_signal(late, inc=1, device_id=(cells, dp), device_id_type=MESH)

    @when(odd == 1, inner_bottom)
    def _():
        answer(block(-2))

    @when(top)
    def _():
        answer(block(2 - COLUMN))

        @pl.when(even)
        def _():
            answer(block(2))
            answer(block(3))

        @when(odd == 1, c >= 6)
        def _():
            for j in range(8):
                answer(block(2), peer(j))

    @when(bottom, odd == 1, jnp.logical_not(first_column))
    def _():
        answer(block(-COLUMN))

    @when(top, even, last_column)
    def _():
        answer(block(COLUMN))
        answer(block(COLUMN + 1))

    def copy(source, target, send, recv, cells, dp):
        return pltpu.make_async_remote_copy(
            src_ref=source, dst_ref=target, send_sem=send, recv_sem=recv,
            device_id=(cells, dp), device_id_type=MESH,
        )

    def coef_copy(j):
        return copy(
            gathered.at[c], gathered.at[c], coef_send.at[j - 1], coef_recv.at[c], peer(j), d
        )

    def in_copy(group, j):
        to = peer(j)
        return copy(
            sens.at[rows_of(group, to), :], slab_in.at[c, slab_rows(group), :],
            in_send.at[group, j - 1], in_recv.at[group, c], to, d,
        )

    for one in own[:3]:
        one.wait()
    for j in range(1, 8):
        coef_copy(j).start()
    for group in range(GROUPS):
        for j in range(1, 8):
            in_copy(group, j).start()

    own[3].wait()
    lane = lax.broadcasted_iota(jnp.int32, (GROUP, CZ), 1)
    line = lax.broadcasted_iota(jnp.int32, (GROUP, CZ), 0)
    chosen = lane == line + c * GROUP

    def arrived(buffer, sem, s):
        return copy(buffer.at[s], buffer.at[s], sem.at[s], sem.at[s], c, d)

    for j in range(1, 8):
        arrived(gathered, coef_recv, peer(j)).wait_recv()
    inner = lax.broadcasted_iota(jnp.int32, (8, CZ), 1) < CZ - 1
    for s in range(8):
        if s < 7:
            coef[s, 0:8, :] = gathered[s, 0:8, :]
        else:
            coef[s, 0:4, :] = gathered[s, 0:4, :]
            coef[s, 4:8, :] = jnp.zeros((4, CZ), jnp.float32)
        coef[s, 8:16, :] = gathered[s, 8:16, :]
        coef[s, 16:24, :] = jnp.where(inner, gathered[s, 16:24, :], 0.0)
    def out_copy(group, j):
        to = peer(j)
        return copy(
            slab_out.at[to, slab_rows(group), :], panels.at[PANEL, rows_of(group, c), :],
            out_send.at[group, j - 1], out_recv.at[group, c], to, d,
        )

    for group in range(GROUPS):
        part_rows = slab_rows(group)
        scaled = jnp.sum(
            jnp.where(chosen, weights[group : group + 1, :], 0.0), axis=1, keepdims=True
        )
        own[4 + group].wait()
        for j in range(1, 8):
            landed = slab_in.at[peer(j), part_rows, :]
            sem = in_recv.at[group, peer(j)]
            copy(landed, landed, sem, sem, c, d).wait_recv()

        def load_in(part, tile, part_rows=part_rows):
            return slab_in[part, part_rows, pl.ds(tile * CZ, CZ)].astype(jnp.float32)

        def store_field(part, tile, value, part_rows=part_rows):
            field[part, part_rows, pl.ds(tile * CZ, CZ)] = value

        def load_field(part, tile, part_rows=part_rows):
            return field[part, part_rows, pl.ds(tile * CZ, CZ)]

        def store_out(part, tile, value, part_rows=part_rows, scaled=scaled):
            slab_out[part, part_rows, pl.ds(tile * CZ, CZ)] = (scaled * value).astype(jnp.bfloat16)

        smoothing_pass(load_in, coef, store_field)
        smoothing_pass(load_field, coef, store_out)

        for j in range(1, 8):
            out_copy(group, j).start()
        panels[PANEL, rows_of(group, c), :] = slab_out[c, part_rows, :]

    first_to = jnp.where(even, block(-2), block(-1))
    first_slot = jnp.where(even, 1, 0)
    chunk = 8 * rows // CHUNKS

    def piece(slot, s):
        return panels.at[slot, pl.ds(s * chunk, chunk), :]

    def first_copy(s):
        return copy(
            piece(PANEL, s), piece(first_slot, s), a_send.at[s], panel_recv.at[first_slot, s], c, first_to
        )

    def second_copy(s):
        return copy(piece(PANEL, s), piece(0, s), b_send.at[s], panel_recv.at[0, s], c, block(2))

    relay_to = jnp.where(bottom, block(COLUMN - 2), block(2 - COLUMN))
    relayed_to = jnp.where(bottom, block(COLUMN), block(-COLUMN - odd))
    relayed_slot = jnp.where(bottom, 0, 1 + odd)

    def to_relay_copy(s, send):
        return copy(
            piece(PANEL, s), relay.at[s // 2], send.at[s], relay_recv.at[s // 2], c, relay_to
        )

    def relayed_copy(i):
        s = 2 * i + 1
        return copy(
            relay.at[i], piece(relayed_slot, s), relay_send.at[i], panel_recv.at[relayed_slot, s], c, relayed_to
        )

    def third_copy(s):
        return copy(piece(PANEL, s), piece(2, s), edge_send.at[s], panel_recv.at[2, s], c, block(-3))

    def pass_relayed():
        for i in range(CHUNKS // 2):
            arrived(relay, relay_recv, i).wait_recv()
            relayed_copy(i).start()

    pl.when(top)(pass_relayed)

    awaited = count(odd == 1, inner_top) + count(bottom) * 2
    awaited += count(bottom, odd == 1) * 2 + count(top, first_column)
    awaited += count(bottom, odd == 1, jnp.logical_not(last_column))

    @pl.when(awaited > 0)
    def _():
        pl.semaphore_wait(late, awaited)

    def passed_copy(s):
        return copy(piece(1, s), piece(1, s), c_send.at[s], panel_recv.at[1, s], c, block(1))

    def panel_arrived(slot, s):
        return copy(
            piece(slot, s), piece(slot, s), panel_recv.at[slot, s], panel_recv.at[slot, s], c, d
        )

    for s in range(CHUNKS):
        group, low = s // 2, s % 2 * 4
        for source in range(low, low + 4):

            @pl.when(c != source)
            def _(group=group, source=source):
                landed = panels.at[PANEL, rows_of(group, source), :]
                sem = out_recv.at[group, source]
                copy(landed, landed, sem, sem, c, d).wait_recv()

        indirect = s % 2 == 1

        up_indirect = jnp.logical_and(top, indirect)
        down_indirect = jnp.logical_and(jnp.logical_and(bottom, even), indirect)

        @when(odd == 1, up_indirect)
        def _(s=s):
            to_relay_copy(s, b_send).start()

        @when(odd == 1, jnp.logical_not(up_indirect))
        def _(s=s):
            second_copy(s).start()

        @pl.when(down_indirect)
        def _(s=s):
            to_relay_copy(s, a_send).start()

        @pl.when(jnp.logical_not(down_indirect))
        def _(s=s):
            first_copy(s).start()

    own_rows = at_rows(c)

    def tile_copy(t, j):
        to = peer(j)
        return copy(
            tiles.at[t, at_rows(to), :], sums.at[t, c], tile_send.at[t, j - 1], tile_recv.at[t, c], to, d
        )

    def tile(left, right, t):
        tiles[t] = lax.dot_general(
            panels[left], panels[right], (((1,), (1,)), ((), ())),
            preferred_element_type=jnp.float32,
        )
        for j in range(1, 8):
            tile_copy(t, j).start()
        sums[t, c] = tiles[t, own_rows, :]

    def final_copy(t, half, to, where):
        return copy(
            reduced.at[t, half], landing.at[own_rows, :], last_send.at[t, half], last_recv.at[c], to, where
        )

    def on_each_half(t, k, where, act, keep):
        for half in range(2):
            to = 2 * k + half
            if where is None:

                @pl.when(c != to)
                def _(half=half, to=to):
                    act(final_copy(t, half, to, d))

                @pl.when(c == to)
                def _(half=half):
                    keep(half)

            else:
                act(final_copy(t, half, to, where))

    def reduce(t, k, where=None):
        for j in range(1, 8):
            s = peer(j)
            copy(sums.at[t, s], sums.at[t, s], tile_recv.at[t, s], tile_recv.at[t, s], c, d).wait_recv()
        value = sums[t, 0]
        for s in range(1, 8):
            value = value + sums[t, s]
        value = value * scale
        reduced[t, 0] = value[:, :CZ]
        reduced[t, 1] = value[:, CZ:]

        def keep(half):
            landing[own_rows, :] = reduced[t, half]

        on_each_half(t, k, where, lambda one: one.start(), keep)

    def end(t, k, where=None):
        for j in range(1, 8):
            tile_copy(t, j).wait_send()
        on_each_half(t, k, where, lambda one: one.wait_send(), lambda half: None)

    tile(PANEL, PANEL, 0)

    @pl.when(even)
    def _():
        for s in range(CHUNKS):
            panel_arrived(0, s).wait_recv()
        tile(PANEL, 0, 1)
        for s in range(CHUNKS):
            panel_arrived(1, s).wait_recv()
            passed_copy(s).start()
        tile(PANEL, 1, 2)
        reduce(0, 0)
        reduce(1, 1)
        for s in range(CHUNKS):
            panel_arrived(2, s).wait_recv()
        tile(PANEL, 2, 3)

        @pl.when(top)
        def _():
            tile(0, 2, 4)

        reduce(2, 2)
        reduce(3, 3)

        @pl.when(top)
        def _():
            reduce(4, 2, block(1))

    @pl.when(odd == 1)
    def _():
        for s in range(CHUNKS):
            indirect = jnp.logical_and(s % 2 == 1, bottom)

            @pl.when(indirect)
            def _(s=s):
                to_relay_copy(s, edge_send).start()

            @pl.when(jnp.logical_not(indirect))
            def _(s=s):
                third_copy(s).start()

        @pl.when(inner_bottom)
        def _():
            for s in range(CHUNKS):
                panel_arrived(0, s).wait_recv()
            tile(0, PANEL, 2)

        for s in range(CHUNKS):
            panel_arrived(1, s).wait_recv()

        @pl.when(bottom)
        def _():
            tile(PANEL, 1, 1)
            pass_relayed()
            reduce(0, 0)
            reduce(1, 1)
            for s in range(CHUNKS):
                panel_arrived(0, s).wait_recv()

        tile(0, 1, 3)

        @pl.when(inner_bottom)
        def _():
            tile(PANEL, 1, 1)
            reduce(0, 0)
            reduce(2, 2, block(-2))

        reduce(3, 3, block(-2))

        @pl.when(inner_bottom)
        def _():
            reduce(1, 1)

    for j in range(1, 8):
        copy(
            landing.at[at_rows(peer(j)), :], landing.at[at_rows(peer(j)), :],
            last_recv.at[peer(j)], last_recv.at[peer(j)], c, d,
        ).wait_recv()

    @when(odd == 1, c >= 4)
    def _():
        copy(
            landing.at[own_rows, :], landing.at[own_rows, :], last_recv.at[c], last_recv.at[c], c, d
        ).wait_recv()

    out[...] = landing[...]

    for j in range(1, 8):
        coef_copy(j).wait_send()
        for group in range(GROUPS):
            in_copy(group, j).wait_send()
            out_copy(group, j).wait_send()
    for s in range(CHUNKS):
        first_copy(s).wait_send()
    end(0, 0)
    end(1, 1)

    @pl.when(jnp.logical_or(top, jnp.logical_and(bottom, odd == 1)))
    def _():
        for i in range(CHUNKS // 2):
            relayed_copy(i).wait_send()

    @pl.when(even)
    def _():
        for s in range(CHUNKS):
            passed_copy(s).wait_send()
        end(2, 2)
        end(3, 3)

        @pl.when(top)
        def _():
            end(4, 2, block(1))

    @pl.when(odd == 1)
    def _():
        for s in range(CHUNKS):
            second_copy(s).wait_send()
            third_copy(s).wait_send()

        @pl.when(inner_bottom)
        def _():
            end(2, 2, block(-2))

        end(3, 3, block(-2))


def body(sensitivity, weights, coef_x, coef_y, coef_z):
    rows, cells = sensitivity.shape
    part = rows // 8
    scale = float(cells * lax.axis_size("cells")) ** (-0.5)
    vmem = pl.BlockSpec(memory_space=pltpu.VMEM)
    dma = pltpu.SemaphoreType.DMA
    return pl.pallas_call(
        functools.partial(kernel, scale),
        out_shape=jax.ShapeDtypeStruct((rows, rows // 2), jnp.float32),
        in_specs=[pl.BlockSpec(memory_space=pl.ANY)] * 5,
        out_specs=vmem,
        scratch_shapes=[
            pltpu.VMEM((2, CZ), jnp.float32),
            pltpu.VMEM((8, 24, CZ), jnp.float32),
            pltpu.VMEM((8, 24, CZ), jnp.float32),
            pltpu.VMEM((8, part, cells), jnp.bfloat16),
            pltpu.VMEM((8, part, cells), jnp.float32),
            pltpu.VMEM((8, part, cells), jnp.bfloat16),
            pltpu.VMEM((4, rows, cells), jnp.bfloat16),
            pltpu.VMEM((5, rows, rows), jnp.float32),
            pltpu.VMEM((5, 8, part, rows), jnp.float32),
            pltpu.VMEM((5, 2, part, CZ), jnp.float32),
            pltpu.VMEM((rows, CZ), jnp.float32),
            pltpu.VMEM((CHUNKS // 2, rows // CHUNKS, cells), jnp.bfloat16),
            dma((7,)), dma((8,)), dma((GROUPS, 7)), dma((GROUPS, 8)), dma((4 + GROUPS,)), dma((GROUPS, 7)), dma((GROUPS, 8)),
            dma((CHUNKS,)), dma((CHUNKS,)), dma((CHUNKS,)), dma((3, CHUNKS)), dma((5, 7)), dma((5, 8)), dma((5, 2)), dma((8,)),
            dma((CHUNKS // 2,)), dma((CHUNKS // 2,)), pltpu.SemaphoreType.REGULAR, dma((CHUNKS,)),
        ],
        compiler_params=pltpu.CompilerParams(
            collective_id=0, has_side_effects=True, vmem_limit_bytes=60 * 1024 * 1024
        ),
        name="gram_band",
    )(
        sensitivity,
        weights.reshape(2, CZ),
        coef_x.reshape(8, CZ),
        coef_y.reshape(8, CZ),
        coef_z.reshape(8, CZ),
    )


def solution(mesh):
    return jax.shard_map(
        body,
        mesh=mesh,
        in_specs=(P("dp", "cells"), P("dp"), P("cells"), P("cells"), P("cells")),
        out_specs=P("dp", "cells"),
        check_vma=False,
    )
```

```python
import functools

import jax
import jax.numpy as jnp
from jax import lax
from jax.experimental import pallas as pl
from jax.experimental.pallas import tpu as pltpu
from jax.sharding import PartitionSpec as P

CY = 4
CZ = 128
GROUP = 16
GROUPS = 2
CHUNKS = 4
COLUMN = 16
MESH = pl.DeviceIdType.MESH
PANEL = 3


def smoothing_pass(load, coef, store):
    def step(part, carry):
        current, entering = carry
        for half in range(2):
            if half == 0:
                above = [load(part, CY + y) for y in range(CY)]
            else:
                upper = jnp.minimum(part + 1, 7)
                above = [load(upper, y) for y in range(CY)]
            flux_x = []
            below_y = None
            for y in range(CY):
                row = half * CY + y
                here = current[y]
                flux = coef[part, pl.ds(row, 1), :] * (above[y] - here)
                change = flux - entering[y]
                flux_x.append(flux)
                if y < CY - 1:
                    flux_y = coef[part, pl.ds(8 + row, 1), :] * (current[y + 1] - here)
                    change = change + flux_y
                if y > 0:
                    change = change - below_y
                below_y = flux_y
                flux_z = coef[part, pl.ds(16 + row, 1), :] * (pltpu.roll(here, CZ - 1, 1) - here)
                change = change + (flux_z - pltpu.roll(flux_z, 1, 1))
                store(part, row, here + change)
            current, entering = tuple(above), tuple(flux_x)
        return current, entering

    first = tuple(load(0, y) for y in range(CY))
    zero = tuple(jnp.zeros((GROUP, CZ), jnp.float32) for _ in range(CY))
    lax.fori_loop(0, 8, step, (first, zero), unroll=4)


def kernel(
    scale, sens, weights_hbm, coef_x, coef_y, coef_z, out,
    weights, gathered, coef, slab_in, field, slab_out, panels, tiles, sums, reduced, landing, far, relay,
    coef_send, coef_recv, in_send, in_recv, own_sem, out_send, out_recv,
    a_send, b_send, c_send, panel_recv, tile_send, tile_recv, last_send, last_recv,
    relay_send, relay_recv, late, edge_send, far_recv,
):
    c = lax.axis_index("cells")
    d = lax.axis_index("dp")
    blocks = lax.axis_size("dp")
    odd = lax.rem(d, 2)
    even = odd == 0
    height = lax.rem(d, COLUMN) // 2
    bottom, top = height == 0, height == COLUMN // 2 - 1
    inner_bottom, inner_top = jnp.logical_not(bottom), jnp.logical_not(top)
    first_column, last_column = d < COLUMN, d >= blocks - COLUMN
    rows = sens.shape[0] // 8

    def block(offset):
        return lax.rem(d + offset + blocks, blocks)

    def peer(j):
        return lax.rem(c + j, 8)

    def at_rows(index):
        return pl.ds(pl.multiple_of(index * rows, rows), rows)


    def rows_of(group, index):
        start = group * (8 * GROUP) + index * GROUP
        return pl.ds(pl.multiple_of(start, GROUP), GROUP)

    def slab_rows(group):
        return pl.ds(group * GROUP, GROUP)

    barrier = pltpu.get_barrier_semaphore()

    def greet(cells, dp):
        pl.semaphore_signal(barrier, inc=1, device_id=(cells, dp), device_id_type=MESH)

    def when(*conditions):
        return pl.when(functools.reduce(jnp.logical_and, conditions))

    for j in range(1, 8):
        greet(peer(j), d)
    greet(c, d + 1 - 2 * odd)

    @when(odd == 1, c >= 4, c < 6, top)
    def _():
        for j in range(1, 8):
            greet(peer(j), block(-1))

    @when(inner_top)
    def _():
        greet(c, block(2))

        @pl.when(even)
        def _():
            greet(c, block(3))

    @when(inner_top, odd == 1, c >= 4)
    def _():
        for j in range(1, 8):
            greet(peer(j), block(2))

    @when(bottom)
    def _():
        greet(c, block(COLUMN - 2))
        greet(c, block(-2))

        @pl.when(odd == 1)
        def _():
            greet(c, block(-3))
            for q in (6, 7):

                @pl.when(c != q)
                def _(q=q):
                    greet(q, block(-2))


    @when(top, even, jnp.logical_not(last_column))
    def _():
        greet(c, block(COLUMN))
        greet(c, block(COLUMN + 1))

    @when(top, first_column)
    def _():
        greet(c, block(-COLUMN - odd))

    own = [
        pltpu.make_async_copy(source, target, own_sem.at[i])
        for i, (source, target) in enumerate(
            [
                (coef_x, gathered.at[c, pl.ds(0, 8), :]),
                (coef_y, gathered.at[c, pl.ds(8, 8), :]),
                (coef_z, gathered.at[c, pl.ds(16, 8), :]),
                (weights_hbm, weights),
            ]
            + [
                (sens.at[rows_of(group, c), :], slab_in.at[c, slab_rows(group), :])
                for group in range(GROUPS)
            ]
        )
    ]
    for one in own:
        one.start()

    def count(*conditions):
        return functools.reduce(jnp.logical_and, conditions).astype(jnp.int32)

    present = 8 + count(odd == 1, inner_bottom) * 4 - count(odd == 1, inner_bottom, c >= 4)
    present += count(top, odd == 1, c >= 6) * 7
    present += count(even, top) * 2 - count(even, top, c >= 4, c < 6)
    present += count(inner_bottom) * (1 + odd)
    present += count(top) * (3 - odd) + count(top, jnp.logical_not(first_column))
    present += count(top, even, last_column) * 2
    pl.semaphore_wait(barrier, present)

    def answer(dp, cells=c):
        pl.semaphore_signal(late, inc=1, device_id=(cells, dp), device_id_type=MESH)

    @when(odd == 1, inner_bottom)
    def _():
        answer(block(-2))

    @when(top)
    def _():
        answer(block(2 - COLUMN))

        @pl.when(even)
        def _():
            answer(block(2))
            answer(block(3))

        @when(odd == 1, c >= 6)
        def _():
            for j in range(8):
                answer(block(2), peer(j))

    @when(top, even, last_column)
    def _():
        answer(block(COLUMN))
        answer(block(COLUMN + 1))

    def copy(source, target, send, recv, cells, dp):
        return pltpu.make_async_remote_copy(
            src_ref=source, dst_ref=target, send_sem=send, recv_sem=recv,
            device_id=(cells, dp), device_id_type=MESH,
        )

    def coef_copy(j):
        return copy(
            gathered.at[c], gathered.at[c], coef_send.at[j - 1], coef_recv.at[c], peer(j), d
        )

    def in_copy(group, j):
        to = peer(j)
        return copy(
            sens.at[rows_of(group, to), :], slab_in.at[c, slab_rows(group), :],
            in_send.at[group, j - 1], in_recv.at[group, c], to, d,
        )

    for one in own[:3]:
        one.wait()
    for j in range(1, 8):
        coef_copy(j).start()
    for group in range(GROUPS):
        for j in range(1, 8):
            in_copy(group, j).start()

    own[3].wait()
    lane = lax.broadcasted_iota(jnp.int32, (GROUP, CZ), 1)
    line = lax.broadcasted_iota(jnp.int32, (GROUP, CZ), 0)
    chosen = lane == line + c * GROUP

    def arrived(buffer, sem, s):
        return copy(buffer.at[s], buffer.at[s], sem.at[s], sem.at[s], c, d)

    for j in range(1, 8):
        arrived(gathered, coef_recv, peer(j)).wait_recv()
    inner = lax.broadcasted_iota(jnp.int32, (8, CZ), 1) < CZ - 1
    for s in range(8):
        if s < 7:
            coef[s, 0:8, :] = gathered[s, 0:8, :]
        else:
            coef[s, 0:4, :] = gathered[s, 0:4, :]
            coef[s, 4:8, :] = jnp.zeros((4, CZ), jnp.float32)
        coef[s, 8:16, :] = gathered[s, 8:16, :]
        coef[s, 16:24, :] = jnp.where(inner, gathered[s, 16:24, :], 0.0)
    def out_copy(group, j):
        to = peer(j)
        return copy(
            slab_out.at[to, slab_rows(group), :], panels.at[PANEL, rows_of(group, c), :],
            out_send.at[group, j - 1], out_recv.at[group, c], to, d,
        )

    for group in range(GROUPS):
        part_rows = slab_rows(group)
        scaled = jnp.sum(
            jnp.where(chosen, weights[group : group + 1, :], 0.0), axis=1, keepdims=True
        )
        own[4 + group].wait()
        for j in range(1, 8):
            landed = slab_in.at[peer(j), part_rows, :]
            sem = in_recv.at[group, peer(j)]
            copy(landed, landed, sem, sem, c, d).wait_recv()

        def load_in(part, tile, part_rows=part_rows):
            return slab_in[part, part_rows, pl.ds(tile * CZ, CZ)].astype(jnp.float32)

        def store_field(part, tile, value, part_rows=part_rows):
            field[part, part_rows, pl.ds(tile * CZ, CZ)] = value

        def load_field(part, tile, part_rows=part_rows):
            return field[part, part_rows, pl.ds(tile * CZ, CZ)]

        def store_out(part, tile, value, part_rows=part_rows, scaled=scaled):
            slab_out[part, part_rows, pl.ds(tile * CZ, CZ)] = (scaled * value).astype(jnp.bfloat16)

        smoothing_pass(load_in, coef, store_field)
        smoothing_pass(load_field, coef, store_out)

        for j in range(1, 8):
            out_copy(group, j).start()
        panels[PANEL, rows_of(group, c), :] = slab_out[c, part_rows, :]

    first_to = jnp.where(even, block(-2), block(-1))
    first_slot = jnp.where(even, 1, 0)
    chunk = 8 * rows // CHUNKS

    def piece(slot, s):
        return panels.at[slot, pl.ds(s * chunk, chunk), :]

    def first_copy(s):
        return copy(
            piece(PANEL, s), piece(first_slot, s), a_send.at[s], panel_recv.at[first_slot, s], c, first_to
        )

    def second_copy(s):
        return copy(piece(PANEL, s), piece(0, s), b_send.at[s], panel_recv.at[0, s], c, block(2))

    relayed_slot = 1 + odd

    def to_relay_copy(s, send):
        return copy(
            piece(PANEL, s), relay.at[s // 2], send.at[s], relay_recv.at[s // 2], c, block(COLUMN - 2)
        )

    def relayed_copy(i):
        s = 2 * i + 1
        return copy(
            relay.at[i], piece(relayed_slot, s), relay_send.at[i], panel_recv.at[relayed_slot, s], c, block(-COLUMN - odd)
        )

    def third_copy(s):
        return copy(piece(PANEL, s), piece(2, s), edge_send.at[s], panel_recv.at[2, s], c, block(-3))

    def pass_relayed(first=0):
        for i in range(first, CHUNKS // 2):
            arrived(relay, relay_recv, i).wait_recv()
            relayed_copy(i).start()

    pl.when(jnp.logical_and(top, even))(pass_relayed)

    awaited = count(odd == 1, inner_top) + count(bottom) * 2
    awaited += count(bottom, odd == 1) * 2 + count(top, first_column)

    @pl.when(awaited > 0)
    def _():
        pl.semaphore_wait(late, awaited)

    def passed_copy(s):
        return copy(piece(1, s), piece(1, s), c_send.at[s], panel_recv.at[1, s], c, block(1))

    def panel_arrived(slot, s):
        return copy(
            piece(slot, s), piece(slot, s), panel_recv.at[slot, s], panel_recv.at[slot, s], c, d
        )

    for s in range(CHUNKS):
        group, low = s // 2, s % 2 * 4
        for source in range(low, low + 4):

            @pl.when(c != source)
            def _(group=group, source=source):
                landed = panels.at[PANEL, rows_of(group, source), :]
                sem = out_recv.at[group, source]
                copy(landed, landed, sem, sem, c, d).wait_recv()

        indirect = s % 2 == 1

        down_indirect = jnp.logical_and(jnp.logical_and(bottom, even), indirect)

        @pl.when(odd == 1)
        def _(s=s):
            second_copy(s).start()

        @pl.when(down_indirect)
        def _(s=s):
            to_relay_copy(s, a_send).start()

        @pl.when(jnp.logical_not(down_indirect))
        def _(s=s):
            first_copy(s).start()

    own_rows = at_rows(c)

    def tile_copy(t, j):
        to = peer(j)
        return copy(
            tiles.at[t, at_rows(to), :], sums.at[t, c], tile_send.at[t, j - 1], tile_recv.at[t, c], to, d
        )

    def form(left, right, t):
        tiles[t] = lax.dot_general(
            panels[left], panels[right], (((1,), (1,)), ((), ())),
            preferred_element_type=jnp.float32,
        )

    def far_copy(half):
        return copy(
            tiles.at[3, :, pl.ds(half * CZ, CZ)], far.at[c], last_send.at[3, half], far_recv.at[c], 6 + half, block(-2)
        )

    def tile(left, right, t):
        form(left, right, t)
        for j in range(1, 8):
            tile_copy(t, j).start()
        sums[t, c] = tiles[t, own_rows, :]

    def final_copy(t, half, to, where):
        return copy(
            reduced.at[t, half], landing.at[own_rows, :], last_send.at[t, half], last_recv.at[c], to, where
        )

    def on_each_half(t, k, where, act, keep):
        for half in range(2):
            to = 2 * k + half
            if where is None:

                @pl.when(c != to)
                def _(half=half, to=to):
                    act(final_copy(t, half, to, d))

                @pl.when(c == to)
                def _(half=half):
                    keep(half)

            else:
                act(final_copy(t, half, to, where))

    def reduce(t, k, where=None):
        for j in range(1, 8):
            s = peer(j)
            copy(sums.at[t, s], sums.at[t, s], tile_recv.at[t, s], tile_recv.at[t, s], c, d).wait_recv()
        value = sums[t, 0]
        for s in range(1, 8):
            value = value + sums[t, s]
        value = value * scale
        reduced[t, 0] = value[:, :CZ]
        reduced[t, 1] = value[:, CZ:]

        def keep(half):
            landing[own_rows, :] = reduced[t, half]

        on_each_half(t, k, where, lambda one: one.start(), keep)

    def end(t, k, where=None):
        for j in range(1, 8):
            tile_copy(t, j).wait_send()
        on_each_half(t, k, where, lambda one: one.wait_send(), lambda half: None)

    tile(PANEL, PANEL, 0)

    @pl.when(even)
    def _():
        for s in range(CHUNKS):
            panel_arrived(0, s).wait_recv()
        tile(PANEL, 0, 1)
        for s in range(CHUNKS):
            panel_arrived(1, s).wait_recv()
            passed_copy(s).start()
        tile(PANEL, 1, 2)
        reduce(0, 0)
        reduce(1, 1)
        for s in range(CHUNKS):
            panel_arrived(2, s).wait_recv()
        tile(PANEL, 2, 3)

        @pl.when(top)
        def _():
            tile(0, 2, 4)

        reduce(2, 2)
        reduce(3, 3)

        @pl.when(top)
        def _():
            reduce(4, 2, block(1))

    @pl.when(odd == 1)
    def _():
        for s in range(CHUNKS):
            indirect = jnp.logical_and(s == CHUNKS - 1, bottom)

            @pl.when(indirect)
            def _(s=s):
                to_relay_copy(s, edge_send).start()

            @pl.when(jnp.logical_not(indirect))
            def _(s=s):
                third_copy(s).start()

        pl.when(top)(functools.partial(pass_relayed, CHUNKS // 2 - 1))

        @pl.when(inner_bottom)
        def _():
            for s in range(CHUNKS):
                panel_arrived(0, s).wait_recv()
            tile(0, PANEL, 2)

        for s in range(CHUNKS):
            panel_arrived(1, s).wait_recv()

        @pl.when(bottom)
        def _():
            tile(PANEL, 1, 1)
            reduce(0, 0)
            reduce(1, 1)
            for s in range(CHUNKS):
                panel_arrived(0, s).wait_recv()
            form(0, 1, 3)
            for half in range(2):
                far_copy(half).start()

        @pl.when(inner_bottom)
        def _():
            tile(PANEL, 1, 1)
            tile(0, 1, 3)
            reduce(0, 0)
            reduce(2, 2, block(-2))
            reduce(1, 1)
            reduce(3, 3, block(-2))

    from_far = functools.reduce(jnp.logical_and, [top, odd == 1, c >= 6])

    @pl.when(from_far)
    def _():
        for s in range(8):
            arrived(far, far_recv, s).wait_recv()
        value = far[0]
        for s in range(1, 8):
            value = value + far[s]
        out[...] = value * scale

    @pl.when(jnp.logical_not(from_far))
    def _():
        def landed(s):
            part = landing.at[at_rows(s), :]
            return copy(part, part, last_recv.at[s], last_recv.at[s], c, d)

        for j in range(1, 8):
            landed(peer(j)).wait_recv()

        @when(odd == 1, c >= 4)
        def _():
            landed(c).wait_recv()

        out[...] = landing[...]

    for j in range(1, 8):
        coef_copy(j).wait_send()
        for group in range(GROUPS):
            in_copy(group, j).wait_send()
            out_copy(group, j).wait_send()
    for s in range(CHUNKS):
        first_copy(s).wait_send()
    end(0, 0)
    end(1, 1)

    @when(top)
    def _():
        relayed_copy(CHUNKS // 2 - 1).wait_send()

        @pl.when(even)
        def _():
            for i in range(CHUNKS // 2 - 1):
                relayed_copy(i).wait_send()

    @pl.when(even)
    def _():
        for s in range(CHUNKS):
            passed_copy(s).wait_send()
        end(2, 2)
        end(3, 3)

        @pl.when(top)
        def _():
            end(4, 2, block(1))

    @pl.when(odd == 1)
    def _():
        for s in range(CHUNKS):
            second_copy(s).wait_send()
            third_copy(s).wait_send()

        @pl.when(inner_bottom)
        def _():
            end(2, 2, block(-2))
            end(3, 3, block(-2))

        @pl.when(bottom)
        def _():
            for half in range(2):
                far_copy(half).wait_send()


def body(sensitivity, weights, coef_x, coef_y, coef_z):
    rows, cells = sensitivity.shape
    part = rows // 8
    scale = float(cells * lax.axis_size("cells")) ** (-0.5)
    vmem = pl.BlockSpec(memory_space=pltpu.VMEM)
    dma = pltpu.SemaphoreType.DMA
    return pl.pallas_call(
        functools.partial(kernel, scale),
        out_shape=jax.ShapeDtypeStruct((rows, rows // 2), jnp.float32),
        in_specs=[pl.BlockSpec(memory_space=pl.ANY)] * 5,
        out_specs=vmem,
        scratch_shapes=[
            pltpu.VMEM((2, CZ), jnp.float32),
            pltpu.VMEM((8, 24, CZ), jnp.float32),
            pltpu.VMEM((8, 24, CZ), jnp.float32),
            pltpu.VMEM((8, part, cells), jnp.bfloat16),
            pltpu.VMEM((8, part, cells), jnp.float32),
            pltpu.VMEM((8, part, cells), jnp.bfloat16),
            pltpu.VMEM((4, rows, cells), jnp.bfloat16),
            pltpu.VMEM((5, rows, rows), jnp.float32),
            pltpu.VMEM((5, 8, part, rows), jnp.float32),
            pltpu.VMEM((5, 2, part, CZ), jnp.float32),
            pltpu.VMEM((rows, CZ), jnp.float32),
            pltpu.VMEM((8, rows, CZ), jnp.float32),
            pltpu.VMEM((CHUNKS // 2, rows // CHUNKS, cells), jnp.bfloat16),
            dma((7,)), dma((8,)), dma((GROUPS, 7)), dma((GROUPS, 8)), dma((4 + GROUPS,)), dma((GROUPS, 7)), dma((GROUPS, 8)),
            dma((CHUNKS,)), dma((CHUNKS,)), dma((CHUNKS,)), dma((3, CHUNKS)), dma((5, 7)), dma((5, 8)), dma((5, 2)), dma((8,)),
            dma((CHUNKS // 2,)), dma((CHUNKS // 2,)), pltpu.SemaphoreType.REGULAR, dma((CHUNKS,)), dma((8,)),
        ],
        compiler_params=pltpu.CompilerParams(
            collective_id=0, has_side_effects=True, vmem_limit_bytes=60 * 1024 * 1024
        ),
        name="gram_band",
    )(
        sensitivity,
        weights.reshape(2, CZ),
        coef_x.reshape(8, CZ),
        coef_y.reshape(8, CZ),
        coef_z.reshape(8, CZ),
    )


def solution(mesh):
    return jax.shard_map(
        body,
        mesh=mesh,
        in_specs=(P("dp", "cells"), P("dp"), P("cells"), P("cells"), P("cells")),
        out_specs=P("dp", "cells"),
        check_vma=False,
    )
```

```python
import functools

import jax
import jax.numpy as jnp
from jax import lax
from jax.experimental import pallas as pl
from jax.experimental.pallas import tpu as pltpu
from jax.sharding import PartitionSpec as P

CY = 4
CZ = 128
GROUP = 16
GROUPS = 2
CHUNKS = 4
COLUMN = 16
MESH = pl.DeviceIdType.MESH
PANEL = 3


def smoothing_pass(load, coef, store):
    def step(part, carry):
        current, entering = carry
        for half in range(2):
            if half == 0:
                above = [load(part, CY + y) for y in range(CY)]
            else:
                upper = jnp.minimum(part + 1, 7)
                above = [load(upper, y) for y in range(CY)]
            flux_x = []
            below_y = None
            for y in range(CY):
                row = half * CY + y
                here = current[y]
                flux = coef[part, pl.ds(row, 1), :] * (above[y] - here)
                change = flux - entering[y]
                flux_x.append(flux)
                if y < CY - 1:
                    flux_y = coef[part, pl.ds(8 + row, 1), :] * (current[y + 1] - here)
                    change = change + flux_y
                if y > 0:
                    change = change - below_y
                below_y = flux_y
                flux_z = coef[part, pl.ds(16 + row, 1), :] * (pltpu.roll(here, CZ - 1, 1) - here)
                change = change + (flux_z - pltpu.roll(flux_z, 1, 1))
                store(part, row, here + change)
            current, entering = tuple(above), tuple(flux_x)
        return current, entering

    first = tuple(load(0, y) for y in range(CY))
    zero = tuple(jnp.zeros((GROUP, CZ), jnp.float32) for _ in range(CY))
    lax.fori_loop(0, 8, step, (first, zero), unroll=4)


def kernel(
    scale, sens, weights_hbm, coef_x, coef_y, coef_z, out,
    weights, gathered, coef, slab_in, field, slab_out, panels, tiles, sums, reduced, landing, far, relay,
    coef_send, coef_recv, in_send, in_recv, own_sem, out_send, out_recv,
    a_send, b_send, c_send, panel_recv, tile_send, tile_recv, last_send, last_recv,
    relay_send, relay_recv, late, edge_send, far_recv, far_send,
):
    c = lax.axis_index("cells")
    d = lax.axis_index("dp")
    blocks = lax.axis_size("dp")
    odd = lax.rem(d, 2)
    even = odd == 0
    height = lax.rem(d, COLUMN) // 2
    bottom, top = height == 0, height == COLUMN // 2 - 1
    inner_bottom, inner_top = jnp.logical_not(bottom), jnp.logical_not(top)
    first_column, last_column = d < COLUMN, d >= blocks - COLUMN
    rows = sens.shape[0] // 8

    def block(offset):
        return lax.rem(d + offset + blocks, blocks)

    def peer(j):
        return lax.rem(c + j, 8)

    def at_rows(index):
        return pl.ds(pl.multiple_of(index * rows, rows), rows)


    def rows_of(group, index):
        start = group * (8 * GROUP) + index * GROUP
        return pl.ds(pl.multiple_of(start, GROUP), GROUP)

    def slab_rows(group):
        return pl.ds(group * GROUP, GROUP)

    barrier = pltpu.get_barrier_semaphore()

    def greet(cells, dp):
        pl.semaphore_signal(barrier, inc=1, device_id=(cells, dp), device_id_type=MESH)

    def when(*conditions):
        return pl.when(functools.reduce(jnp.logical_and, conditions))

    for j in range(1, 8):
        greet(peer(j), d)
    greet(c, d + 1 - 2 * odd)

    @when(odd == 1, c >= 4, c < 6, top)
    def _():
        for j in range(1, 8):
            greet(peer(j), block(-1))

    @when(inner_top)
    def _():
        greet(c, block(2))

        @pl.when(even)
        def _():
            greet(c, block(3))

    @when(inner_top, odd == 1, c >= 4)
    def _():
        for j in range(1, 8):
            greet(peer(j), block(2))

    @when(bottom)
    def _():
        greet(c, block(COLUMN - 2))
        greet(c, block(-2))

        @pl.when(odd == 1)
        def _():
            greet(c, block(-3))
            for q in (6, 7):

                @pl.when(c != q)
                def _(q=q):
                    greet(q, block(-2))


    @when(top, even, jnp.logical_not(last_column))
    def _():
        greet(c, block(COLUMN))
        greet(c, block(COLUMN + 1))

    @when(top, first_column)
    def _():
        greet(c, block(-COLUMN - odd))

    own = [
        pltpu.make_async_copy(source, target, own_sem.at[i])
        for i, (source, target) in enumerate(
            [
                (coef_x, gathered.at[c, pl.ds(0, 8), :]),
                (coef_y, gathered.at[c, pl.ds(8, 8), :]),
                (coef_z, gathered.at[c, pl.ds(16, 8), :]),
                (weights_hbm, weights),
            ]
            + [
                (sens.at[rows_of(group, c), :], slab_in.at[c, slab_rows(group), :])
                for group in range(GROUPS)
            ]
        )
    ]
    for one in own:
        one.start()

    def count(*conditions):
        return functools.reduce(jnp.logical_and, conditions).astype(jnp.int32)

    present = 8 + count(odd == 1, inner_bottom) * 4 - count(odd == 1, inner_bottom, c >= 4)
    present += count(top, odd == 1, c >= 6) * 7
    present += count(even, top) * 2 - count(even, top, c >= 4, c < 6)
    present += count(inner_bottom) * (1 + odd)
    present += count(top) * (3 - odd) + count(top, jnp.logical_not(first_column))
    present += count(top, even, last_column) * 2
    pl.semaphore_wait(barrier, present)

    def answer(dp, cells=c):
        pl.semaphore_signal(late, inc=1, device_id=(cells, dp), device_id_type=MESH)

    @when(odd == 1, inner_bottom)
    def _():
        answer(block(-2))

    @when(top)
    def _():
        answer(block(2 - COLUMN))

        @pl.when(even)
        def _():
            answer(block(2))
            answer(block(3))

        @when(odd == 1, c >= 6)
        def _():
            for j in range(8):
                answer(block(2), peer(j))

    @when(top, even, last_column)
    def _():
        answer(block(COLUMN))
        answer(block(COLUMN + 1))

    def copy(source, target, send, recv, cells, dp):
        return pltpu.make_async_remote_copy(
            src_ref=source, dst_ref=target, send_sem=send, recv_sem=recv,
            device_id=(cells, dp), device_id_type=MESH,
        )

    def coef_copy(j):
        return copy(
            gathered.at[c], gathered.at[c], coef_send.at[j - 1], coef_recv.at[c], peer(j), d
        )

    def in_copy(group, j):
        to = peer(j)
        return copy(
            sens.at[rows_of(group, to), :], slab_in.at[c, slab_rows(group), :],
            in_send.at[group, j - 1], in_recv.at[group, c], to, d,
        )

    for one in own[:3]:
        one.wait()
    for j in range(1, 8):
        coef_copy(j).start()
    for group in range(GROUPS):
        for j in range(1, 8):
            in_copy(group, j).start()

    own[3].wait()
    lane = lax.broadcasted_iota(jnp.int32, (GROUP, CZ), 1)
    line = lax.broadcasted_iota(jnp.int32, (GROUP, CZ), 0)
    chosen = lane == line + c * GROUP

    def arrived(buffer, sem, s):
        return copy(buffer.at[s], buffer.at[s], sem.at[s], sem.at[s], c, d)

    for j in range(1, 8):
        arrived(gathered, coef_recv, peer(j)).wait_recv()
    inner = lax.broadcasted_iota(jnp.int32, (8, CZ), 1) < CZ - 1
    for s in range(8):
        if s < 7:
            coef[s, 0:8, :] = gathered[s, 0:8, :]
        else:
            coef[s, 0:4, :] = gathered[s, 0:4, :]
            coef[s, 4:8, :] = jnp.zeros((4, CZ), jnp.float32)
        coef[s, 8:16, :] = gathered[s, 8:16, :]
        coef[s, 16:24, :] = jnp.where(inner, gathered[s, 16:24, :], 0.0)
    def out_copy(group, j):
        to = peer(j)
        return copy(
            slab_out.at[to, slab_rows(group), :], panels.at[PANEL, rows_of(group, c), :],
            out_send.at[group, j - 1], out_recv.at[group, c], to, d,
        )

    for group in range(GROUPS):
        part_rows = slab_rows(group)
        scaled = jnp.sum(
            jnp.where(chosen, weights[group : group + 1, :], 0.0), axis=1, keepdims=True
        )
        own[4 + group].wait()
        for j in range(1, 8):
            landed = slab_in.at[peer(j), part_rows, :]
            sem = in_recv.at[group, peer(j)]
            copy(landed, landed, sem, sem, c, d).wait_recv()

        def load_in(part, tile, part_rows=part_rows):
            return slab_in[part, part_rows, pl.ds(tile * CZ, CZ)].astype(jnp.float32)

        def store_field(part, tile, value, part_rows=part_rows):
            field[part, part_rows, pl.ds(tile * CZ, CZ)] = value

        def load_field(part, tile, part_rows=part_rows):
            return field[part, part_rows, pl.ds(tile * CZ, CZ)]

        def store_out(part, tile, value, part_rows=part_rows, scaled=scaled):
            slab_out[part, part_rows, pl.ds(tile * CZ, CZ)] = (scaled * value).astype(jnp.bfloat16)

        smoothing_pass(load_in, coef, store_field)
        smoothing_pass(load_field, coef, store_out)

        for j in range(1, 8):
            out_copy(group, j).start()
        panels[PANEL, rows_of(group, c), :] = slab_out[c, part_rows, :]

    first_to = jnp.where(even, block(-2), block(-1))
    first_slot = jnp.where(even, 1, 0)
    chunk = 8 * rows // CHUNKS

    def piece(slot, s):
        return panels.at[slot, pl.ds(s * chunk, chunk), :]

    def first_copy(s):
        return copy(
            piece(PANEL, s), piece(first_slot, s), a_send.at[s], panel_recv.at[first_slot, s], c, first_to
        )

    def second_copy(s):
        return copy(piece(PANEL, s), piece(0, s), b_send.at[s], panel_recv.at[0, s], c, block(2))

    relayed_slot = 1 + odd

    def to_relay_copy(s, send):
        return copy(
            piece(PANEL, s), relay.at[s // 2], send.at[s], relay_recv.at[s // 2], c, block(COLUMN - 2)
        )

    def relayed_copy(i):
        s = 2 * i + 1
        return copy(
            relay.at[i], piece(relayed_slot, s), relay_send.at[i], panel_recv.at[relayed_slot, s], c, block(-COLUMN - odd)
        )

    def third_copy(s):
        return copy(piece(PANEL, s), piece(2, s), edge_send.at[s], panel_recv.at[2, s], c, block(-3))

    def pass_relayed(first=0):
        for i in range(first, CHUNKS // 2):
            arrived(relay, relay_recv, i).wait_recv()
            relayed_copy(i).start()

    pl.when(jnp.logical_and(top, even))(pass_relayed)

    awaited = count(odd == 1, inner_top) + count(bottom) * 2
    awaited += count(bottom, odd == 1) * 2 + count(top, first_column)

    @pl.when(awaited > 0)
    def _():
        pl.semaphore_wait(late, awaited)

    def passed_copy(s):
        return copy(piece(1, s), piece(1, s), c_send.at[s], panel_recv.at[1, s], c, block(1))

    def panel_arrived(slot, s):
        return copy(
            piece(slot, s), piece(slot, s), panel_recv.at[slot, s], panel_recv.at[slot, s], c, d
        )

    for s in range(CHUNKS):
        group, low = s // 2, s % 2 * 4
        for source in range(low, low + 4):

            @pl.when(c != source)
            def _(group=group, source=source):
                landed = panels.at[PANEL, rows_of(group, source), :]
                sem = out_recv.at[group, source]
                copy(landed, landed, sem, sem, c, d).wait_recv()

        indirect = s % 2 == 1

        down_indirect = jnp.logical_and(jnp.logical_and(bottom, even), indirect)

        @pl.when(odd == 1)
        def _(s=s):
            second_copy(s).start()

        @pl.when(down_indirect)
        def _(s=s):
            to_relay_copy(s, a_send).start()

        @pl.when(jnp.logical_not(down_indirect))
        def _(s=s):
            first_copy(s).start()

    own_rows = at_rows(c)

    def tile_copy(t, j):
        to = peer(j)
        return copy(
            tiles.at[t, at_rows(to), :], sums.at[t, c], tile_send.at[t, j - 1], tile_recv.at[t, c], to, d
        )

    def form(left, right, t):
        tiles[t] = lax.dot_general(
            panels[left], panels[right], (((1,), (1,)), ((), ())),
            preferred_element_type=jnp.float32,
        )

    def far_copy(t, half, first, where):
        return copy(
            tiles.at[t, :, pl.ds(half * CZ, CZ)], far.at[c], far_send.at[half], far_recv.at[c], first + half, where
        )

    def far_tile(left, right, t, first, where):
        form(left, right, t)
        for half in range(2):
            far_copy(t, half, first, where).start()

    def tile(left, right, t):
        form(left, right, t)
        for j in range(1, 8):
            tile_copy(t, j).start()
        sums[t, c] = tiles[t, own_rows, :]

    def final_copy(t, half, to, where):
        return copy(
            reduced.at[t, half], landing.at[own_rows, :], last_send.at[t, half], last_recv.at[c], to, where
        )

    def on_each_half(t, k, where, act, keep):
        for half in range(2):
            to = 2 * k + half
            if where is None:

                @pl.when(c != to)
                def _(half=half, to=to):
                    act(final_copy(t, half, to, d))

                @pl.when(c == to)
                def _(half=half):
                    keep(half)

            else:
                act(final_copy(t, half, to, where))

    def reduce(t, k, where=None):
        for j in range(1, 8):
            s = peer(j)
            copy(sums.at[t, s], sums.at[t, s], tile_recv.at[t, s], tile_recv.at[t, s], c, d).wait_recv()
        value = sums[t, 0]
        for s in range(1, 8):
            value = value + sums[t, s]
        value = value * scale
        reduced[t, 0] = value[:, :CZ]
        reduced[t, 1] = value[:, CZ:]

        def keep(half):
            landing[own_rows, :] = reduced[t, half]

        on_each_half(t, k, where, lambda one: one.start(), keep)

    def end(t, k, where=None):
        for j in range(1, 8):
            tile_copy(t, j).wait_send()
        on_each_half(t, k, where, lambda one: one.wait_send(), lambda half: None)

    tile(PANEL, PANEL, 0)

    @pl.when(even)
    def _():
        for s in range(CHUNKS):
            panel_arrived(0, s).wait_recv()
        tile(PANEL, 0, 1)
        for s in range(CHUNKS):
            panel_arrived(1, s).wait_recv()
            passed_copy(s).start()
        tile(PANEL, 1, 2)
        reduce(0, 0)
        reduce(1, 1)
        for s in range(CHUNKS):
            panel_arrived(2, s).wait_recv()
        tile(PANEL, 2, 3)

        @pl.when(top)
        def _():
            far_tile(0, 2, 4, 4, block(1))

        reduce(2, 2)
        reduce(3, 3)

    @pl.when(odd == 1)
    def _():
        for s in range(CHUNKS):
            indirect = jnp.logical_and(s == CHUNKS - 1, bottom)

            @pl.when(indirect)
            def _(s=s):
                to_relay_copy(s, edge_send).start()

            @pl.when(jnp.logical_not(indirect))
            def _(s=s):
                third_copy(s).start()

        pl.when(top)(functools.partial(pass_relayed, CHUNKS // 2 - 1))

        @pl.when(inner_bottom)
        def _():
            for s in range(CHUNKS):
                panel_arrived(0, s).wait_recv()
            tile(0, PANEL, 2)

        for s in range(CHUNKS):
            panel_arrived(1, s).wait_recv()

        @pl.when(bottom)
        def _():
            tile(PANEL, 1, 1)
            reduce(0, 0)
            reduce(1, 1)
            for s in range(CHUNKS):
                panel_arrived(0, s).wait_recv()
            far_tile(0, 1, 3, 6, block(-2))

        @pl.when(inner_bottom)
        def _():
            tile(PANEL, 1, 1)
            tile(0, 1, 3)
            reduce(0, 0)
            reduce(2, 2, block(-2))
            reduce(1, 1)
            reduce(3, 3, block(-2))

    from_far = functools.reduce(jnp.logical_and, [top, odd == 1, c >= 4])

    @pl.when(from_far)
    def _():
        for s in range(8):
            arrived(far, far_recv, s).wait_recv()
        value = far[0]
        for s in range(1, 8):
            value = value + far[s]
        out[...] = value * scale

    @pl.when(jnp.logical_not(from_far))
    def _():
        def landed(s):
            part = landing.at[at_rows(s), :]
            return copy(part, part, last_recv.at[s], last_recv.at[s], c, d)

        for j in range(1, 8):
            landed(peer(j)).wait_recv()

        @when(odd == 1, c >= 4)
        def _():
            landed(c).wait_recv()

        out[...] = landing[...]

    for j in range(1, 8):
        coef_copy(j).wait_send()
        for group in range(GROUPS):
            in_copy(group, j).wait_send()
            out_copy(group, j).wait_send()
    for s in range(CHUNKS):
        first_copy(s).wait_send()
    end(0, 0)
    end(1, 1)

    @when(top)
    def _():
        relayed_copy(CHUNKS // 2 - 1).wait_send()

        @pl.when(even)
        def _():
            for i in range(CHUNKS // 2 - 1):
                relayed_copy(i).wait_send()

    @pl.when(even)
    def _():
        for s in range(CHUNKS):
            passed_copy(s).wait_send()
        end(2, 2)
        end(3, 3)

        @pl.when(top)
        def _():
            for half in range(2):
                far_copy(4, half, 4, block(1)).wait_send()

    @pl.when(odd == 1)
    def _():
        for s in range(CHUNKS):
            second_copy(s).wait_send()
            third_copy(s).wait_send()

        @pl.when(inner_bottom)
        def _():
            end(2, 2, block(-2))
            end(3, 3, block(-2))

        @pl.when(bottom)
        def _():
            for half in range(2):
                far_copy(3, half, 6, block(-2)).wait_send()


def body(sensitivity, weights, coef_x, coef_y, coef_z):
    rows, cells = sensitivity.shape
    part = rows // 8
    scale = float(cells * lax.axis_size("cells")) ** (-0.5)
    vmem = pl.BlockSpec(memory_space=pltpu.VMEM)
    dma = pltpu.SemaphoreType.DMA
    return pl.pallas_call(
        functools.partial(kernel, scale),
        out_shape=jax.ShapeDtypeStruct((rows, rows // 2), jnp.float32),
        in_specs=[pl.BlockSpec(memory_space=pl.ANY)] * 5,
        out_specs=vmem,
        scratch_shapes=[
            pltpu.VMEM((2, CZ), jnp.float32),
            pltpu.VMEM((8, 24, CZ), jnp.float32),
            pltpu.VMEM((8, 24, CZ), jnp.float32),
            pltpu.VMEM((8, part, cells), jnp.bfloat16),
            pltpu.VMEM((8, part, cells), jnp.float32),
            pltpu.VMEM((8, part, cells), jnp.bfloat16),
            pltpu.VMEM((4, rows, cells), jnp.bfloat16),
            pltpu.VMEM((5, rows, rows), jnp.float32),
            pltpu.VMEM((4, 8, part, rows), jnp.float32),
            pltpu.VMEM((4, 2, part, CZ), jnp.float32),
            pltpu.VMEM((rows, CZ), jnp.float32),
            pltpu.VMEM((8, rows, CZ), jnp.float32),
            pltpu.VMEM((CHUNKS // 2, rows // CHUNKS, cells), jnp.bfloat16),
            dma((7,)), dma((8,)), dma((GROUPS, 7)), dma((GROUPS, 8)), dma((4 + GROUPS,)), dma((GROUPS, 7)), dma((GROUPS, 8)),
            dma((CHUNKS,)), dma((CHUNKS,)), dma((CHUNKS,)), dma((3, CHUNKS)), dma((4, 7)), dma((4, 8)), dma((4, 2)), dma((8,)),
            dma((CHUNKS // 2,)), dma((CHUNKS // 2,)), pltpu.SemaphoreType.REGULAR, dma((CHUNKS,)), dma((8,)), dma((2,)),
        ],
        compiler_params=pltpu.CompilerParams(
            collective_id=0, has_side_effects=True, vmem_limit_bytes=60 * 1024 * 1024
        ),
        name="gram_band",
    )(
        sensitivity,
        weights.reshape(2, CZ),
        coef_x.reshape(8, CZ),
        coef_y.reshape(8, CZ),
        coef_z.reshape(8, CZ),
    )


def solution(mesh):
    return jax.shard_map(
        body,
        mesh=mesh,
        in_specs=(P("dp", "cells"), P("dp"), P("cells"), P("cells"), P("cells")),
        out_specs=P("dp", "cells"),
        check_vma=False,
    )
```

```python
import functools

import jax
import jax.numpy as jnp
from jax import lax
from jax.experimental import pallas as pl
from jax.experimental.pallas import tpu as pltpu
from jax.sharding import PartitionSpec as P

CY = 4
CZ = 128
GROUP = 16
GROUPS = 2
CHUNKS = 4
COLUMN = 16
MESH = pl.DeviceIdType.MESH
PANEL = 3


def smoothing_pass(load, coef, store):
    def step(part, carry):
        current, entering = carry
        for half in range(2):
            if half == 0:
                above = [load(part, CY + y) for y in range(CY)]
            else:
                upper = jnp.minimum(part + 1, 7)
                above = [load(upper, y) for y in range(CY)]
            flux_x = []
            below_y = None
            for y in range(CY):
                row = half * CY + y
                here = current[y]
                flux = coef[part, pl.ds(row, 1), :] * (above[y] - here)
                change = flux - entering[y]
                flux_x.append(flux)
                if y < CY - 1:
                    flux_y = coef[part, pl.ds(8 + row, 1), :] * (current[y + 1] - here)
                    change = change + flux_y
                if y > 0:
                    change = change - below_y
                below_y = flux_y
                flux_z = coef[part, pl.ds(16 + row, 1), :] * (pltpu.roll(here, CZ - 1, 1) - here)
                change = change + (flux_z - pltpu.roll(flux_z, 1, 1))
                store(part, row, here + change)
            current, entering = tuple(above), tuple(flux_x)
        return current, entering

    first = tuple(load(0, y) for y in range(CY))
    zero = tuple(jnp.zeros((GROUP, CZ), jnp.float32) for _ in range(CY))
    lax.fori_loop(0, 8, step, (first, zero), unroll=4)


def kernel(
    scale, sens, weights_hbm, coef_x, coef_y, coef_z, out,
    weights, gathered, coef, slab_in, field, slab_out, panels, tiles, sums, reduced, landing, far, relay,
    coef_send, coef_recv, in_send, in_recv, own_sem, out_send, out_recv,
    a_send, b_send, c_send, panel_recv, tile_send, tile_recv, last_send, last_recv,
    relay_send, relay_recv, late, edge_send, far_recv, far_send, across_send,
):
    c = lax.axis_index("cells")
    d = lax.axis_index("dp")
    blocks = lax.axis_size("dp")
    odd = lax.rem(d, 2)
    even = odd == 0
    height = lax.rem(d, COLUMN) // 2
    bottom, top = height == 0, height == COLUMN // 2 - 1
    inner_bottom, inner_top = jnp.logical_not(bottom), jnp.logical_not(top)
    first_column, last_column = d < COLUMN, d >= blocks - COLUMN
    rows = sens.shape[0] // 8

    def block(offset):
        return lax.rem(d + offset + blocks, blocks)

    def peer(j):
        return lax.rem(c + j, 8)

    def at_rows(index):
        return pl.ds(pl.multiple_of(index * rows, rows), rows)


    def rows_of(group, index):
        start = group * (8 * GROUP) + index * GROUP
        return pl.ds(pl.multiple_of(start, GROUP), GROUP)

    def slab_rows(group):
        return pl.ds(group * GROUP, GROUP)

    barrier = pltpu.get_barrier_semaphore()

    def greet(cells, dp):
        pl.semaphore_signal(barrier, inc=1, device_id=(cells, dp), device_id_type=MESH)

    def when(*conditions):
        return pl.when(functools.reduce(jnp.logical_and, conditions))

    for j in range(1, 8):
        greet(peer(j), d)
    greet(c, d + 1 - 2 * odd)

    @when(odd == 1, c >= 4, c < 6, top)
    def _():
        for j in range(1, 8):
            greet(peer(j), block(-1))

    @when(inner_top)
    def _():
        greet(c, block(2))

        @pl.when(even)
        def _():
            greet(c, block(3))

    @when(inner_top, odd == 1, c >= 4)
    def _():
        for j in range(1, 8):
            greet(peer(j), block(2))

    @when(bottom)
    def _():
        greet(c, block(COLUMN - 2))
        greet(c, block(-2))

        @pl.when(odd == 1)
        def _():
            greet(c, block(-3))
            for j in range(1, 8):
                greet(peer(j), block(-2))

        @when(odd == 1, jnp.logical_not(last_column))
        def _():
            greet(c, block(COLUMN))


    @when(top, even, jnp.logical_not(last_column))
    def _():
        greet(c, block(COLUMN))
        greet(c, block(COLUMN + 1))

    @when(top, first_column)
    def _():
        greet(c, block(-COLUMN - odd))

    own = [
        pltpu.make_async_copy(source, target, own_sem.at[i])
        for i, (source, target) in enumerate(
            [
                (coef_x, gathered.at[c, pl.ds(0, 8), :]),
                (coef_y, gathered.at[c, pl.ds(8, 8), :]),
                (coef_z, gathered.at[c, pl.ds(16, 8), :]),
                (weights_hbm, weights),
            ]
            + [
                (sens.at[rows_of(group, c), :], slab_in.at[c, slab_rows(group), :])
                for group in range(GROUPS)
            ]
        )
    ]
    for one in own:
        one.start()

    def count(*conditions):
        return functools.reduce(jnp.logical_and, conditions).astype(jnp.int32)

    present = 8 + count(odd == 1, inner_bottom) * 4 - count(odd == 1, inner_bottom, c >= 4)
    present += count(top, odd == 1) * 7
    present += count(bottom, odd == 1, jnp.logical_not(first_column))
    present += count(even, top) * 2 - count(even, top, c >= 4, c < 6)
    present += count(inner_bottom) * (1 + odd)
    present += count(top) * (3 - odd) + count(top, jnp.logical_not(first_column))
    present += count(top, even, last_column) * 2
    pl.semaphore_wait(barrier, present)

    def answer(dp, cells=c):
        pl.semaphore_signal(late, inc=1, device_id=(cells, dp), device_id_type=MESH)

    @when(odd == 1, inner_bottom)
    def _():
        answer(block(-2))

    @when(top)
    def _():
        answer(block(2 - COLUMN))

        @pl.when(even)
        def _():
            answer(block(2))
            answer(block(3))

        @pl.when(odd == 1)
        def _():
            for j in range(8):
                answer(block(2), peer(j))

    @when(bottom, odd == 1, jnp.logical_not(first_column))
    def _():
        answer(block(-COLUMN))

    @when(top, even, last_column)
    def _():
        answer(block(COLUMN))
        answer(block(COLUMN + 1))

    def copy(source, target, send, recv, cells, dp):
        return pltpu.make_async_remote_copy(
            src_ref=source, dst_ref=target, send_sem=send, recv_sem=recv,
            device_id=(cells, dp), device_id_type=MESH,
        )

    def coef_copy(j):
        return copy(
            gathered.at[c], gathered.at[c], coef_send.at[j - 1], coef_recv.at[c], peer(j), d
        )

    def in_copy(group, j):
        to = peer(j)
        return copy(
            sens.at[rows_of(group, to), :], slab_in.at[c, slab_rows(group), :],
            in_send.at[group, j - 1], in_recv.at[group, c], to, d,
        )

    for one in own[:3]:
        one.wait()
    for j in range(1, 8):
        coef_copy(j).start()
    for group in range(GROUPS):
        for j in range(1, 8):
            in_copy(group, j).start()

    own[3].wait()
    lane = lax.broadcasted_iota(jnp.int32, (GROUP, CZ), 1)
    line = lax.broadcasted_iota(jnp.int32, (GROUP, CZ), 0)
    chosen = lane == line + c * GROUP

    def arrived(buffer, sem, s):
        return copy(buffer.at[s], buffer.at[s], sem.at[s], sem.at[s], c, d)

    for j in range(1, 8):
        arrived(gathered, coef_recv, peer(j)).wait_recv()
    inner = lax.broadcasted_iota(jnp.int32, (8, CZ), 1) < CZ - 1
    for s in range(8):
        if s < 7:
            coef[s, 0:8, :] = gathered[s, 0:8, :]
        else:
            coef[s, 0:4, :] = gathered[s, 0:4, :]
            coef[s, 4:8, :] = jnp.zeros((4, CZ), jnp.float32)
        coef[s, 8:16, :] = gathered[s, 8:16, :]
        coef[s, 16:24, :] = jnp.where(inner, gathered[s, 16:24, :], 0.0)
    def out_copy(group, j):
        to = peer(j)
        return copy(
            slab_out.at[to, slab_rows(group), :], panels.at[PANEL, rows_of(group, c), :],
            out_send.at[group, j - 1], out_recv.at[group, c], to, d,
        )

    for group in range(GROUPS):
        part_rows = slab_rows(group)
        scaled = jnp.sum(
            jnp.where(chosen, weights[group : group + 1, :], 0.0), axis=1, keepdims=True
        )
        own[4 + group].wait()
        for j in range(1, 8):
            landed = slab_in.at[peer(j), part_rows, :]
            sem = in_recv.at[group, peer(j)]
            copy(landed, landed, sem, sem, c, d).wait_recv()

        def load_in(part, tile, part_rows=part_rows):
            return slab_in[part, part_rows, pl.ds(tile * CZ, CZ)].astype(jnp.float32)

        def store_field(part, tile, value, part_rows=part_rows):
            field[part, part_rows, pl.ds(tile * CZ, CZ)] = value

        def load_field(part, tile, part_rows=part_rows):
            return field[part, part_rows, pl.ds(tile * CZ, CZ)]

        def store_out(part, tile, value, part_rows=part_rows, scaled=scaled):
            slab_out[part, part_rows, pl.ds(tile * CZ, CZ)] = (scaled * value).astype(jnp.bfloat16)

        smoothing_pass(load_in, coef, store_field)
        smoothing_pass(load_field, coef, store_out)

        for j in range(1, 8):
            out_copy(group, j).start()
        panels[PANEL, rows_of(group, c), :] = slab_out[c, part_rows, :]

    first_to = jnp.where(even, block(-2), block(-1))
    first_slot = jnp.where(even, 1, 0)
    chunk = 8 * rows // CHUNKS

    def piece(slot, s):
        return panels.at[slot, pl.ds(s * chunk, chunk), :]

    def first_copy(s):
        return copy(
            piece(PANEL, s), piece(first_slot, s), a_send.at[s], panel_recv.at[first_slot, s], c, first_to
        )

    def second_copy(s):
        return copy(piece(PANEL, s), piece(0, s), b_send.at[s], panel_recv.at[0, s], c, block(2))

    relay_to = jnp.where(bottom, block(COLUMN - 2), block(2 - COLUMN))
    relayed_to = jnp.where(bottom, block(COLUMN), block(-COLUMN - odd))
    relayed_slot = jnp.where(bottom, 0, 1 + odd)

    def to_relay_copy(s, send):
        return copy(
            piece(PANEL, s), relay.at[s // 2], send.at[s], relay_recv.at[s // 2], c, relay_to
        )

    def relayed_copy(i):
        s = 2 * i + 1
        return copy(
            relay.at[i], piece(relayed_slot, s), relay_send.at[i], panel_recv.at[relayed_slot, s], c, relayed_to
        )

    def third_copy(s):
        return copy(piece(PANEL, s), piece(2, s), edge_send.at[s], panel_recv.at[2, s], c, block(-3))

    def pass_relayed(first=0):
        for i in range(first, CHUNKS // 2):
            arrived(relay, relay_recv, i).wait_recv()
            relayed_copy(i).start()

    pl.when(jnp.logical_and(top, even))(pass_relayed)

    awaited = count(odd == 1, inner_top) + count(bottom) * 2
    awaited += count(bottom, odd == 1) * 8 + count(top, first_column)
    awaited += count(bottom, odd == 1, jnp.logical_not(last_column))

    @pl.when(awaited > 0)
    def _():
        pl.semaphore_wait(late, awaited)

    def passed_copy(s):
        return copy(piece(1, s), piece(1, s), c_send.at[s], panel_recv.at[1, s], c, block(1))

    def panel_arrived(slot, s):
        return copy(
            piece(slot, s), piece(slot, s), panel_recv.at[slot, s], panel_recv.at[slot, s], c, d
        )

    for s in range(CHUNKS):
        group, low = s // 2, s % 2 * 4
        for source in range(low, low + 4):

            @pl.when(c != source)
            def _(group=group, source=source):
                landed = panels.at[PANEL, rows_of(group, source), :]
                sem = out_recv.at[group, source]
                copy(landed, landed, sem, sem, c, d).wait_recv()

        indirect = s % 2 == 1

        down_indirect = jnp.logical_and(jnp.logical_and(bottom, even), indirect)

        up_indirect = functools.reduce(jnp.logical_and, [top, indirect, jnp.logical_not(last_column)])

        @when(odd == 1, up_indirect)
        def _(s=s):
            to_relay_copy(s, b_send).start()

        @when(odd == 1, jnp.logical_not(up_indirect))
        def _(s=s):
            second_copy(s).start()

        @pl.when(down_indirect)
        def _(s=s):
            to_relay_copy(s, a_send).start()

        @pl.when(jnp.logical_not(down_indirect))
        def _(s=s):
            first_copy(s).start()

    own_rows = at_rows(c)

    def tile_copy(t, j):
        to = peer(j)
        return copy(
            tiles.at[t, at_rows(to), :], sums.at[t, c], tile_send.at[t, j - 1], tile_recv.at[t, c], to, d
        )

    def form(left, right, t):
        tiles[t] = lax.dot_general(
            panels[left], panels[right], (((1,), (1,)), ((), ())),
            preferred_element_type=jnp.float32,
        )

    def far_copy(t, half, first, where):
        return copy(
            tiles.at[t, :, pl.ds(half * CZ, CZ)], far.at[c], far_send.at[half], far_recv.at[c], first + half, where
        )

    def far_tile(left, right, t, first, where):
        form(left, right, t)
        for half in range(2):
            far_copy(t, half, first, where).start()

    def across_copy(j):
        to = peer(j)
        return copy(
            tiles.at[3, at_rows(to), :], sums.at[4, c], across_send.at[j], tile_recv.at[4, c], to, block(-2)
        )

    def tile(left, right, t):
        form(left, right, t)
        for j in range(1, 8):
            tile_copy(t, j).start()
        sums[t, c] = tiles[t, own_rows, :]

    def final_copy(t, half, to, where):
        return copy(
            reduced.at[t, half], landing.at[own_rows, :], last_send.at[t, half], last_recv.at[c], to, where
        )

    def on_each_half(t, k, where, act, keep):
        for half in range(2):
            to = 2 * k + half
            if where is None:

                @pl.when(c != to)
                def _(half=half, to=to):
                    act(final_copy(t, half, to, d))

                @pl.when(c == to)
                def _(half=half):
                    keep(half)

            else:
                act(final_copy(t, half, to, where))

    def reduce(t, k, where=None, first=1):
        for j in range(first, 8):
            s = peer(j)
            copy(sums.at[t, s], sums.at[t, s], tile_recv.at[t, s], tile_recv.at[t, s], c, d).wait_recv()
        value = sums[t, 0]
        for s in range(1, 8):
            value = value + sums[t, s]
        value = value * scale
        reduced[t, 0] = value[:, :CZ]
        reduced[t, 1] = value[:, CZ:]

        def keep(half):
            landing[own_rows, :] = reduced[t, half]

        on_each_half(t, k, where, lambda one: one.start(), keep)

    def end(t, k, where=None):
        for j in range(1, 8):
            tile_copy(t, j).wait_send()
        on_each_half(t, k, where, lambda one: one.wait_send(), lambda half: None)

    @pl.when(odd == 1)
    def _():
        for s in range(CHUNKS):
            indirect = jnp.logical_and(s == CHUNKS - 1, bottom)

            @pl.when(indirect)
            def _(s=s):
                to_relay_copy(s, edge_send).start()

            @pl.when(jnp.logical_not(indirect))
            def _(s=s):
                third_copy(s).start()

    tile(PANEL, PANEL, 0)

    @pl.when(even)
    def _():
        for s in range(CHUNKS):
            panel_arrived(0, s).wait_recv()
        tile(PANEL, 0, 1)
        for s in range(CHUNKS):
            panel_arrived(1, s).wait_recv()
            passed_copy(s).start()
        tile(PANEL, 1, 2)
        reduce(0, 0)
        reduce(1, 1)
        for s in range(CHUNKS):
            panel_arrived(2, s).wait_recv()
        tile(PANEL, 2, 3)

        @pl.when(top)
        def _():
            far_tile(0, 2, 4, 4, block(1))

        reduce(2, 2)
        reduce(3, 3)

    @pl.when(odd == 1)
    def _():

        pl.when(top)(functools.partial(pass_relayed, CHUNKS // 2 - 1))

        @pl.when(inner_bottom)
        def _():
            for s in range(CHUNKS):
                panel_arrived(0, s).wait_recv()
            tile(0, PANEL, 2)

        for s in range(CHUNKS):
            panel_arrived(1, s).wait_recv()

        @pl.when(bottom)
        def _():
            tile(PANEL, 1, 1)
            pl.when(jnp.logical_not(last_column))(pass_relayed)
            reduce(0, 0)
            reduce(1, 1)
            for s in range(CHUNKS):
                panel_arrived(0, s).wait_recv()
            form(0, 1, 3)
            for j in range(8):
                across_copy(j).start()

        @pl.when(inner_bottom)
        def _():
            tile(PANEL, 1, 1)
            tile(0, 1, 3)
            reduce(0, 0)
            reduce(2, 2, block(-2))
            reduce(1, 1)
            reduce(3, 3, block(-2))

        @pl.when(top)
        def _():
            reduce(4, 3, first=0)

    from_far = functools.reduce(jnp.logical_and, [top, odd == 1, c >= 4, c < 6])

    @pl.when(from_far)
    def _():
        for s in range(8):
            arrived(far, far_recv, s).wait_recv()
        value = far[0]
        for s in range(1, 8):
            value = value + far[s]
        out[...] = value * scale

    @pl.when(jnp.logical_not(from_far))
    def _():
        def landed(s):
            part = landing.at[at_rows(s), :]
            return copy(part, part, last_recv.at[s], last_recv.at[s], c, d)

        for j in range(1, 8):
            landed(peer(j)).wait_recv()

        @when(odd == 1, c >= 4, inner_top)
        def _():
            landed(c).wait_recv()

        out[...] = landing[...]

    for j in range(1, 8):
        coef_copy(j).wait_send()
        for group in range(GROUPS):
            in_copy(group, j).wait_send()
            out_copy(group, j).wait_send()
    for s in range(CHUNKS):
        first_copy(s).wait_send()
    end(0, 0)
    end(1, 1)

    @when(bottom, odd == 1, jnp.logical_not(last_column))
    def _():
        for i in range(CHUNKS // 2):
            relayed_copy(i).wait_send()

    @when(top)
    def _():
        relayed_copy(CHUNKS // 2 - 1).wait_send()

        @pl.when(even)
        def _():
            for i in range(CHUNKS // 2 - 1):
                relayed_copy(i).wait_send()

    @pl.when(even)
    def _():
        for s in range(CHUNKS):
            passed_copy(s).wait_send()
        end(2, 2)
        end(3, 3)

        @pl.when(top)
        def _():
            for half in range(2):
                far_copy(4, half, 4, block(1)).wait_send()

    @pl.when(odd == 1)
    def _():
        for s in range(CHUNKS):
            second_copy(s).wait_send()
            third_copy(s).wait_send()

        @pl.when(inner_bottom)
        def _():
            end(2, 2, block(-2))
            end(3, 3, block(-2))

        @pl.when(bottom)
        def _():
            for j in range(8):
                across_copy(j).wait_send()

        @pl.when(top)
        def _():
            on_each_half(4, 3, None, lambda one: one.wait_send(), lambda half: None)


def body(sensitivity, weights, coef_x, coef_y, coef_z):
    rows, cells = sensitivity.shape
    part = rows // 8
    scale = float(cells * lax.axis_size("cells")) ** (-0.5)
    vmem = pl.BlockSpec(memory_space=pltpu.VMEM)
    dma = pltpu.SemaphoreType.DMA
    return pl.pallas_call(
        functools.partial(kernel, scale),
        out_shape=jax.ShapeDtypeStruct((rows, rows // 2), jnp.float32),
        in_specs=[pl.BlockSpec(memory_space=pl.ANY)] * 5,
        out_specs=vmem,
        scratch_shapes=[
            pltpu.VMEM((2, CZ), jnp.float32),
            pltpu.VMEM((8, 24, CZ), jnp.float32),
            pltpu.VMEM((8, 24, CZ), jnp.float32),
            pltpu.VMEM((8, part, cells), jnp.bfloat16),
            pltpu.VMEM((8, part, cells), jnp.float32),
            pltpu.VMEM((8, part, cells), jnp.bfloat16),
            pltpu.VMEM((4, rows, cells), jnp.bfloat16),
            pltpu.VMEM((5, rows, rows), jnp.float32),
            pltpu.VMEM((5, 8, part, rows), jnp.float32),
            pltpu.VMEM((5, 2, part, CZ), jnp.float32),
            pltpu.VMEM((rows, CZ), jnp.float32),
            pltpu.VMEM((8, rows, CZ), jnp.float32),
            pltpu.VMEM((CHUNKS // 2, rows // CHUNKS, cells), jnp.bfloat16),
            dma((7,)), dma((8,)), dma((GROUPS, 7)), dma((GROUPS, 8)), dma((4 + GROUPS,)), dma((GROUPS, 7)), dma((GROUPS, 8)),
            dma((CHUNKS,)), dma((CHUNKS,)), dma((CHUNKS,)), dma((3, CHUNKS)), dma((4, 7)), dma((5, 8)), dma((5, 2)), dma((8,)),
            dma((CHUNKS // 2,)), dma((CHUNKS // 2,)), pltpu.SemaphoreType.REGULAR, dma((CHUNKS,)), dma((8,)), dma((2,)), dma((8,)),
        ],
        compiler_params=pltpu.CompilerParams(
            collective_id=0, has_side_effects=True, vmem_limit_bytes=60 * 1024 * 1024
        ),
        name="gram_band",
    )(
        sensitivity,
        weights.reshape(2, CZ),
        coef_x.reshape(8, CZ),
        coef_y.reshape(8, CZ),
        coef_z.reshape(8, CZ),
    )


def solution(mesh):
    return jax.shard_map(
        body,
        mesh=mesh,
        in_specs=(P("dp", "cells"), P("dp"), P("cells"), P("cells"), P("cells")),
        out_specs=P("dp", "cells"),
        check_vma=False,
    )
```

```python
import functools

import jax
import jax.numpy as jnp
from jax import lax
from jax.experimental import pallas as pl
from jax.experimental.pallas import tpu as pltpu
from jax.sharding import PartitionSpec as P

CY = 4
CZ = 128
GROUP = 16
GROUPS = 2
CHUNKS = 4
COLUMN = 16
MESH = pl.DeviceIdType.MESH
PANEL = 3


def smoothing_pass(load, coef, store):
    def step(part, carry):
        current, entering = carry
        for half in range(2):
            if half == 0:
                above = [load(part, CY + y) for y in range(CY)]
            else:
                upper = jnp.minimum(part + 1, 7)
                above = [load(upper, y) for y in range(CY)]
            flux_x = []
            below_y = None
            for y in range(CY):
                row = half * CY + y
                here = current[y]
                flux = coef[part, pl.ds(row, 1), :] * (above[y] - here)
                change = flux - entering[y]
                flux_x.append(flux)
                if y < CY - 1:
                    flux_y = coef[part, pl.ds(8 + row, 1), :] * (current[y + 1] - here)
                    change = change + flux_y
                if y > 0:
                    change = change - below_y
                below_y = flux_y
                flux_z = coef[part, pl.ds(16 + row, 1), :] * (pltpu.roll(here, CZ - 1, 1) - here)
                change = change + (flux_z - pltpu.roll(flux_z, 1, 1))
                store(part, row, here + change)
            current, entering = tuple(above), tuple(flux_x)
        return current, entering

    first = tuple(load(0, y) for y in range(CY))
    zero = tuple(jnp.zeros((GROUP, CZ), jnp.float32) for _ in range(CY))
    lax.fori_loop(0, 8, step, (first, zero), unroll=4)


def kernel(
    scale, sens, weights_hbm, coef_x, coef_y, coef_z, out,
    weights, gathered, coef, slab_in, field, slab_out, panels, tiles, sums, reduced, landing, far, relay,
    coef_send, coef_recv, in_send, in_recv, own_sem, out_send, out_recv,
    a_send, b_send, c_send, panel_recv, tile_send, tile_recv, last_send, last_recv,
    relay_send, relay_recv, late, edge_send, far_recv, far_send, across_send,
):
    c = lax.axis_index("cells")
    d = lax.axis_index("dp")
    blocks = lax.axis_size("dp")
    odd = lax.rem(d, 2)
    even = odd == 0
    height = lax.rem(d, COLUMN) // 2
    bottom, top = height == 0, height == COLUMN // 2 - 1
    inner_bottom, inner_top = jnp.logical_not(bottom), jnp.logical_not(top)
    first_column, last_column = d < COLUMN, d >= blocks - COLUMN
    rows = sens.shape[0] // 8

    def block(offset):
        return lax.rem(d + offset + blocks, blocks)

    def peer(j):
        return lax.rem(c + j, 8)

    def at_rows(index):
        return pl.ds(pl.multiple_of(index * rows, rows), rows)


    def rows_of(group, index):
        start = group * (8 * GROUP) + index * GROUP
        return pl.ds(pl.multiple_of(start, GROUP), GROUP)

    def slab_rows(group):
        return pl.ds(group * GROUP, GROUP)

    own = [
        pltpu.make_async_copy(source, target, own_sem.at[i])
        for i, (source, target) in enumerate(
            [
                (coef_x, gathered.at[c, pl.ds(0, 8), :]),
                (coef_y, gathered.at[c, pl.ds(8, 8), :]),
                (coef_z, gathered.at[c, pl.ds(16, 8), :]),
                (weights_hbm, weights),
            ]
            + [
                (sens.at[rows_of(group, c), :], slab_in.at[c, slab_rows(group), :])
                for group in range(GROUPS)
            ]
        )
    ]
    for one in own:
        one.start()

    barrier = pltpu.get_barrier_semaphore()

    def greet(cells, dp):
        pl.semaphore_signal(barrier, inc=1, device_id=(cells, dp), device_id_type=MESH)

    def when(*conditions):
        return pl.when(functools.reduce(jnp.logical_and, conditions))

    for j in range(1, 8):
        greet(peer(j), d)
    greet(c, d + 1 - 2 * odd)

    @when(odd == 1, c >= 4, c < 6, top)
    def _():
        for j in range(1, 8):
            greet(peer(j), block(-1))

    @when(inner_top)
    def _():
        greet(c, block(2))

        @pl.when(even)
        def _():
            greet(c, block(3))

    @when(inner_top, odd == 1, c >= 4)
    def _():
        for j in range(1, 8):
            greet(peer(j), block(2))

    @when(bottom)
    def _():
        greet(c, block(COLUMN - 2))
        greet(c, block(-2))

        @pl.when(odd == 1)
        def _():
            greet(c, block(-3))
            for j in range(1, 8):
                greet(peer(j), block(-2))

        @when(odd == 1, jnp.logical_not(last_column))
        def _():
            greet(c, block(COLUMN))


    @when(top, even, jnp.logical_not(last_column))
    def _():
        greet(c, block(COLUMN))
        greet(c, block(COLUMN + 1))

    @when(top, first_column)
    def _():
        greet(c, block(-COLUMN - odd))


    def count(*conditions):
        return functools.reduce(jnp.logical_and, conditions).astype(jnp.int32)

    present = 8 + count(odd == 1, inner_bottom) * 4 - count(odd == 1, inner_bottom, c >= 4)
    present += count(top, odd == 1) * 7
    present += count(bottom, odd == 1, jnp.logical_not(first_column))
    present += count(even, top) * 2 - count(even, top, c >= 4, c < 6)
    present += count(inner_bottom) * (1 + odd)
    present += count(top) * (3 - odd) + count(top, jnp.logical_not(first_column))
    present += count(top, even, last_column) * 2
    pl.semaphore_wait(barrier, present)

    def answer(dp, cells=c):
        pl.semaphore_signal(late, inc=1, device_id=(cells, dp), device_id_type=MESH)

    @when(odd == 1, inner_bottom)
    def _():
        answer(block(-2))

    @when(top)
    def _():
        answer(block(2 - COLUMN))

        @pl.when(even)
        def _():
            answer(block(2))
            answer(block(3))

        @pl.when(odd == 1)
        def _():
            for j in range(8):
                answer(block(2), peer(j))

    @when(bottom, odd == 1, jnp.logical_not(first_column))
    def _():
        answer(block(-COLUMN))

    @when(top, even, last_column)
    def _():
        answer(block(COLUMN))
        answer(block(COLUMN + 1))

    def copy(source, target, send, recv, cells, dp):
        return pltpu.make_async_remote_copy(
            src_ref=source, dst_ref=target, send_sem=send, recv_sem=recv,
            device_id=(cells, dp), device_id_type=MESH,
        )

    def coef_copy(j):
        return copy(
            gathered.at[c], gathered.at[c], coef_send.at[j - 1], coef_recv.at[c], peer(j), d
        )

    def in_copy(group, j):
        to = peer(j)
        return copy(
            sens.at[rows_of(group, to), :], slab_in.at[c, slab_rows(group), :],
            in_send.at[group, j - 1], in_recv.at[group, c], to, d,
        )

    for one in own[:3]:
        one.wait()
    for j in range(1, 8):
        coef_copy(j).start()
    for group in range(GROUPS):
        for j in range(1, 8):
            in_copy(group, j).start()

    own[3].wait()
    lane = lax.broadcasted_iota(jnp.int32, (GROUP, CZ), 1)
    line = lax.broadcasted_iota(jnp.int32, (GROUP, CZ), 0)
    chosen = lane == line + c * GROUP

    def arrived(buffer, sem, s):
        return copy(buffer.at[s], buffer.at[s], sem.at[s], sem.at[s], c, d)

    for j in range(1, 8):
        arrived(gathered, coef_recv, peer(j)).wait_recv()
    inner = lax.broadcasted_iota(jnp.int32, (8, CZ), 1) < CZ - 1
    for s in range(8):
        if s < 7:
            coef[s, 0:8, :] = gathered[s, 0:8, :]
        else:
            coef[s, 0:4, :] = gathered[s, 0:4, :]
            coef[s, 4:8, :] = jnp.zeros((4, CZ), jnp.float32)
        coef[s, 8:16, :] = gathered[s, 8:16, :]
        coef[s, 16:24, :] = jnp.where(inner, gathered[s, 16:24, :], 0.0)
    def out_copy(group, j):
        to = peer(j)
        return copy(
            slab_out.at[to, slab_rows(group), :], panels.at[PANEL, rows_of(group, c), :],
            out_send.at[group, j - 1], out_recv.at[group, c], to, d,
        )

    for group in range(GROUPS):
        part_rows = slab_rows(group)
        scaled = jnp.sum(
            jnp.where(chosen, weights[group : group + 1, :], 0.0), axis=1, keepdims=True
        )
        own[4 + group].wait()
        for j in range(1, 8):
            landed = slab_in.at[peer(j), part_rows, :]
            sem = in_recv.at[group, peer(j)]
            copy(landed, landed, sem, sem, c, d).wait_recv()

        def load_in(part, tile, part_rows=part_rows):
            return slab_in[part, part_rows, pl.ds(tile * CZ, CZ)].astype(jnp.float32)

        def store_field(part, tile, value, part_rows=part_rows):
            field[part, part_rows, pl.ds(tile * CZ, CZ)] = value

        def load_field(part, tile, part_rows=part_rows):
            return field[part, part_rows, pl.ds(tile * CZ, CZ)]

        def store_out(part, tile, value, part_rows=part_rows, scaled=scaled):
            slab_out[part, part_rows, pl.ds(tile * CZ, CZ)] = (scaled * value).astype(jnp.bfloat16)

        smoothing_pass(load_in, coef, store_field)
        smoothing_pass(load_field, coef, store_out)

        for j in range(1, 8):
            out_copy(group, j).start()
        panels[PANEL, rows_of(group, c), :] = slab_out[c, part_rows, :]

    first_to = jnp.where(even, block(-2), block(-1))
    first_slot = jnp.where(even, 1, 0)
    chunk = 8 * rows // CHUNKS

    def piece(slot, s):
        return panels.at[slot, pl.ds(s * chunk, chunk), :]

    def first_copy(s):
        return copy(
            piece(PANEL, s), piece(first_slot, s), a_send.at[s], panel_recv.at[first_slot, s], c, first_to
        )

    def second_copy(s):
        return copy(piece(PANEL, s), piece(0, s), b_send.at[s], panel_recv.at[0, s], c, block(2))

    relay_to = jnp.where(bottom, block(COLUMN - 2), block(2 - COLUMN))
    relayed_to = jnp.where(bottom, block(COLUMN), block(-COLUMN - odd))
    relayed_slot = jnp.where(bottom, 0, 1 + odd)

    def to_relay_copy(s, send):
        return copy(
            piece(PANEL, s), relay.at[s // 2], send.at[s], relay_recv.at[s // 2], c, relay_to
        )

    def relayed_copy(i):
        s = 2 * i + 1
        return copy(
            relay.at[i], piece(relayed_slot, s), relay_send.at[i], panel_recv.at[relayed_slot, s], c, relayed_to
        )

    def third_copy(s):
        return copy(piece(PANEL, s), piece(2, s), edge_send.at[s], panel_recv.at[2, s], c, block(-3))

    def pass_relayed(first=0):
        for i in range(first, CHUNKS // 2):
            arrived(relay, relay_recv, i).wait_recv()
            relayed_copy(i).start()

    pl.when(jnp.logical_and(top, even))(pass_relayed)

    awaited = count(odd == 1, inner_top) + count(bottom) * 2
    awaited += count(bottom, odd == 1) * 8 + count(top, first_column)
    awaited += count(bottom, odd == 1, jnp.logical_not(last_column))

    @pl.when(awaited > 0)
    def _():
        pl.semaphore_wait(late, awaited)

    def passed_copy(s):
        return copy(piece(1, s), piece(1, s), c_send.at[s], panel_recv.at[1, s], c, block(1))

    def panel_arrived(slot, s):
        return copy(
            piece(slot, s), piece(slot, s), panel_recv.at[slot, s], panel_recv.at[slot, s], c, d
        )

    for s in range(CHUNKS):
        group, low = s // 2, s % 2 * 4
        for source in range(low, low + 4):

            @pl.when(c != source)
            def _(group=group, source=source):
                landed = panels.at[PANEL, rows_of(group, source), :]
                sem = out_recv.at[group, source]
                copy(landed, landed, sem, sem, c, d).wait_recv()

        indirect = s % 2 == 1

        down_indirect = jnp.logical_and(jnp.logical_and(bottom, even), indirect)

        up_indirect = functools.reduce(jnp.logical_and, [top, indirect, jnp.logical_not(last_column)])

        @when(odd == 1, up_indirect)
        def _(s=s):
            to_relay_copy(s, b_send).start()

        @when(odd == 1, jnp.logical_not(up_indirect))
        def _(s=s):
            second_copy(s).start()

        @pl.when(down_indirect)
        def _(s=s):
            to_relay_copy(s, a_send).start()

        @pl.when(jnp.logical_not(down_indirect))
        def _(s=s):
            first_copy(s).start()

    own_rows = at_rows(c)

    def tile_copy(t, j):
        to = peer(j)
        return copy(
            tiles.at[t, at_rows(to), :], sums.at[t, c], tile_send.at[t, j - 1], tile_recv.at[t, c], to, d
        )

    def form(left, right, t):
        tiles[t] = lax.dot_general(
            panels[left], panels[right], (((1,), (1,)), ((), ())),
            preferred_element_type=jnp.float32,
        )

    def far_copy(t, half, first, where):
        return copy(
            tiles.at[t, :, pl.ds(half * CZ, CZ)], far.at[c], far_send.at[half], far_recv.at[c], first + half, where
        )

    def far_tile(left, right, t, first, where):
        form(left, right, t)
        for half in range(2):
            far_copy(t, half, first, where).start()

    def across_copy(j):
        to = peer(j)
        return copy(
            tiles.at[3, at_rows(to), :], sums.at[4, c], across_send.at[j], tile_recv.at[4, c], to, block(-2)
        )

    def tile(left, right, t):
        form(left, right, t)
        for j in range(1, 8):
            tile_copy(t, j).start()
        sums[t, c] = tiles[t, own_rows, :]

    def final_copy(t, half, to, where):
        return copy(
            reduced.at[t, half], landing.at[own_rows, :], last_send.at[t, half], last_recv.at[c], to, where
        )

    def on_each_half(t, k, where, act, keep):
        for half in range(2):
            to = 2 * k + half
            if where is None:

                @pl.when(c != to)
                def _(half=half, to=to):
                    act(final_copy(t, half, to, d))

                @pl.when(c == to)
                def _(half=half):
                    keep(half)

            else:
                act(final_copy(t, half, to, where))

    def reduce(t, k, where=None, first=1):
        for j in range(first, 8):
            s = peer(j)
            copy(sums.at[t, s], sums.at[t, s], tile_recv.at[t, s], tile_recv.at[t, s], c, d).wait_recv()
        value = sums[t, 0]
        for s in range(1, 8):
            value = value + sums[t, s]
        value = value * scale
        reduced[t, 0] = value[:, :CZ]
        reduced[t, 1] = value[:, CZ:]

        def keep(half):
            landing[own_rows, :] = reduced[t, half]

        on_each_half(t, k, where, lambda one: one.start(), keep)

    def end(t, k, where=None):
        for j in range(1, 8):
            tile_copy(t, j).wait_send()
        on_each_half(t, k, where, lambda one: one.wait_send(), lambda half: None)

    @pl.when(odd == 1)
    def _():
        for s in range(CHUNKS):
            indirect = jnp.logical_and(s == CHUNKS - 1, bottom)

            @pl.when(indirect)
            def _(s=s):
                to_relay_copy(s, edge_send).start()

            @pl.when(jnp.logical_not(indirect))
            def _(s=s):
                third_copy(s).start()

    tile(PANEL, PANEL, 0)

    @pl.when(even)
    def _():
        for s in range(CHUNKS):
            panel_arrived(0, s).wait_recv()
        tile(PANEL, 0, 1)
        for s in range(CHUNKS):
            panel_arrived(1, s).wait_recv()
            passed_copy(s).start()
        tile(PANEL, 1, 2)
        reduce(0, 0)
        reduce(1, 1)
        for s in range(CHUNKS):
            panel_arrived(2, s).wait_recv()
        tile(PANEL, 2, 3)

        @pl.when(top)
        def _():
            far_tile(0, 2, 4, 4, block(1))

        reduce(2, 2)
        reduce(3, 3)

    @pl.when(odd == 1)
    def _():

        pl.when(top)(functools.partial(pass_relayed, CHUNKS // 2 - 1))

        @pl.when(inner_bottom)
        def _():
            for s in range(CHUNKS):
                panel_arrived(0, s).wait_recv()
            tile(0, PANEL, 2)

        for s in range(CHUNKS):
            panel_arrived(1, s).wait_recv()

        @pl.when(bottom)
        def _():
            tile(PANEL, 1, 1)
            pl.when(jnp.logical_not(last_column))(pass_relayed)
            reduce(0, 0)
            reduce(1, 1)
            for s in range(CHUNKS):
                panel_arrived(0, s).wait_recv()
            form(0, 1, 3)
            for j in range(8):
                across_copy(j).start()

        @pl.when(inner_bottom)
        def _():
            tile(PANEL, 1, 1)
            tile(0, 1, 3)
            reduce(0, 0)
            reduce(2, 2, block(-2))
            reduce(1, 1)
            reduce(3, 3, block(-2))

        @pl.when(top)
        def _():
            reduce(4, 3, first=0)

    from_far = functools.reduce(jnp.logical_and, [top, odd == 1, c >= 4, c < 6])

    @pl.when(from_far)
    def _():
        for s in range(8):
            arrived(far, far_recv, s).wait_recv()
        value = far[0]
        for s in range(1, 8):
            value = value + far[s]
        landing[...] = value * scale

    @pl.when(jnp.logical_not(from_far))
    def _():
        def landed(s):
            part = landing.at[at_rows(s), :]
            return copy(part, part, last_recv.at[s], last_recv.at[s], c, d)

        for j in range(1, 8):
            landed(peer(j)).wait_recv()

        @when(odd == 1, c >= 4, inner_top)
        def _():
            landed(c).wait_recv()


    final = pltpu.make_async_copy(landing, out, own_sem.at[0])
    final.start()

    for j in range(1, 8):
        coef_copy(j).wait_send()
        for group in range(GROUPS):
            in_copy(group, j).wait_send()
            out_copy(group, j).wait_send()
    for s in range(CHUNKS):
        first_copy(s).wait_send()
    end(0, 0)
    end(1, 1)

    @when(bottom, odd == 1, jnp.logical_not(last_column))
    def _():
        for i in range(CHUNKS // 2):
            relayed_copy(i).wait_send()

    @when(top)
    def _():
        relayed_copy(CHUNKS // 2 - 1).wait_send()

        @pl.when(even)
        def _():
            for i in range(CHUNKS // 2 - 1):
                relayed_copy(i).wait_send()

    @pl.when(even)
    def _():
        for s in range(CHUNKS):
            passed_copy(s).wait_send()
        end(2, 2)
        end(3, 3)

        @pl.when(top)
        def _():
            for half in range(2):
                far_copy(4, half, 4, block(1)).wait_send()

    @pl.when(odd == 1)
    def _():
        for s in range(CHUNKS):
            second_copy(s).wait_send()
            third_copy(s).wait_send()

        @pl.when(inner_bottom)
        def _():
            end(2, 2, block(-2))
            end(3, 3, block(-2))

        @pl.when(bottom)
        def _():
            for j in range(8):
                across_copy(j).wait_send()

        @pl.when(top)
        def _():
            on_each_half(4, 3, None, lambda one: one.wait_send(), lambda half: None)

    final.wait()


def body(sensitivity, weights, coef_x, coef_y, coef_z):
    rows, cells = sensitivity.shape
    part = rows // 8
    scale = float(cells * lax.axis_size("cells")) ** (-0.5)
    dma = pltpu.SemaphoreType.DMA
    return pl.pallas_call(
        functools.partial(kernel, scale),
        out_shape=jax.ShapeDtypeStruct((rows, rows // 2), jnp.float32),
        in_specs=[pl.BlockSpec(memory_space=pl.ANY)] * 5,
        out_specs=pl.BlockSpec(memory_space=pl.ANY),
        scratch_shapes=[
            pltpu.VMEM((2, CZ), jnp.float32),
            pltpu.VMEM((8, 24, CZ), jnp.float32),
            pltpu.VMEM((8, 24, CZ), jnp.float32),
            pltpu.VMEM((8, part, cells), jnp.bfloat16),
            pltpu.VMEM((8, part, cells), jnp.float32),
            pltpu.VMEM((8, part, cells), jnp.bfloat16),
            pltpu.VMEM((4, rows, cells), jnp.bfloat16),
            pltpu.VMEM((5, rows, rows), jnp.float32),
            pltpu.VMEM((5, 8, part, rows), jnp.float32),
            pltpu.VMEM((5, 2, part, CZ), jnp.float32),
            pltpu.VMEM((rows, CZ), jnp.float32),
            pltpu.VMEM((8, rows, CZ), jnp.float32),
            pltpu.VMEM((CHUNKS // 2, rows // CHUNKS, cells), jnp.bfloat16),
            dma((7,)), dma((8,)), dma((GROUPS, 7)), dma((GROUPS, 8)), dma((4 + GROUPS,)), dma((GROUPS, 7)), dma((GROUPS, 8)),
            dma((CHUNKS,)), dma((CHUNKS,)), dma((CHUNKS,)), dma((3, CHUNKS)), dma((4, 7)), dma((5, 8)), dma((5, 2)), dma((8,)),
            dma((CHUNKS // 2,)), dma((CHUNKS // 2,)), pltpu.SemaphoreType.REGULAR, dma((CHUNKS,)), dma((8,)), dma((2,)), dma((8,)),
        ],
        compiler_params=pltpu.CompilerParams(
            collective_id=0, has_side_effects=True, vmem_limit_bytes=60 * 1024 * 1024
        ),
        name="gram_band",
    )(
        sensitivity,
        weights.reshape(2, CZ),
        coef_x.reshape(8, CZ),
        coef_y.reshape(8, CZ),
        coef_z.reshape(8, CZ),
    )


def solution(mesh):
    return jax.shard_map(
        body,
        mesh=mesh,
        in_specs=(P("dp", "cells"), P("dp"), P("cells"), P("cells"), P("cells")),
        out_specs=P("dp", "cells"),
        check_vma=False,
    )
```

```python
import functools

import jax
import jax.numpy as jnp
from jax import lax
from jax.experimental import pallas as pl
from jax.experimental.pallas import tpu as pltpu
from jax.sharding import PartitionSpec as P

CY = 4
CZ = 128
GROUP = 16
GROUPS = 2
CHUNKS = 4
COLUMN = 16
MESH = pl.DeviceIdType.MESH
PANEL = 3


def smoothing_pass(load, coef, store):
    def step(part, carry):
        current, entering = carry
        for half in range(2):
            if half == 0:
                above = [load(part, CY + y) for y in range(CY)]
            else:
                upper = jnp.minimum(part + 1, 7)
                above = [load(upper, y) for y in range(CY)]
            flux_x = []
            below_y = None
            for y in range(CY):
                row = half * CY + y
                here = current[y]
                flux = coef[part, pl.ds(row, 1), :] * (above[y] - here)
                change = flux - entering[y]
                flux_x.append(flux)
                if y < CY - 1:
                    flux_y = coef[part, pl.ds(8 + row, 1), :] * (current[y + 1] - here)
                    change = change + flux_y
                if y > 0:
                    change = change - below_y
                below_y = flux_y
                flux_z = coef[part, pl.ds(16 + row, 1), :] * (pltpu.roll(here, CZ - 1, 1) - here)
                change = change + (flux_z - pltpu.roll(flux_z, 1, 1))
                store(part, row, here + change)
            current, entering = tuple(above), tuple(flux_x)
        return current, entering

    first = tuple(load(0, y) for y in range(CY))
    zero = tuple(jnp.zeros((GROUP, CZ), jnp.float32) for _ in range(CY))
    lax.fori_loop(0, 8, step, (first, zero), unroll=4)


def kernel(
    scale, sens, weights_hbm, coef_x, coef_y, coef_z, out,
    weights, gathered, coef, slab_in, field, slab_out, panels, tiles, sums, reduced, landing, far, relay,
    coef_send, coef_recv, in_send, in_recv, own_sem, out_send, out_recv,
    a_send, b_send, c_send, panel_recv, tile_send, tile_recv, last_send, last_recv,
    relay_send, relay_recv, late, edge_send, far_recv, far_send, across_send,
):
    c = lax.axis_index("cells")
    d = lax.axis_index("dp")
    blocks = lax.axis_size("dp")
    odd = lax.rem(d, 2)
    even = odd == 0
    height = lax.rem(d, COLUMN) // 2
    bottom, top = height == 0, height == COLUMN // 2 - 1
    inner_bottom, inner_top = jnp.logical_not(bottom), jnp.logical_not(top)
    first_column, last_column = d < COLUMN, d >= blocks - COLUMN
    rows = sens.shape[0] // 8

    def block(offset):
        return lax.rem(d + offset + blocks, blocks)

    def peer(j):
        return lax.rem(c + j, 8)

    def at_rows(index):
        return pl.ds(pl.multiple_of(index * rows, rows), rows)


    def rows_of(group, index):
        start = group * (8 * GROUP) + index * GROUP
        return pl.ds(pl.multiple_of(start, GROUP), GROUP)

    def slab_rows(group):
        return pl.ds(group * GROUP, GROUP)

    own = [
        pltpu.make_async_copy(source, target, own_sem.at[i])
        for i, (source, target) in enumerate(
            [
                (coef_x, gathered.at[c, pl.ds(0, 8), :]),
                (coef_y, gathered.at[c, pl.ds(8, 8), :]),
                (coef_z, gathered.at[c, pl.ds(16, 8), :]),
                (weights_hbm, weights),
            ]
            + [
                (sens.at[rows_of(group, c), :], slab_in.at[c, slab_rows(group), :])
                for group in range(GROUPS)
            ]
        )
    ]
    for one in own:
        one.start()

    barrier = pltpu.get_barrier_semaphore()

    def greet(cells, dp):
        pl.semaphore_signal(barrier, inc=1, device_id=(cells, dp), device_id_type=MESH)

    def when(*conditions):
        return pl.when(functools.reduce(jnp.logical_and, conditions))

    for j in range(1, 8):
        greet(peer(j), d)
    greet(c, d + 1 - 2 * odd)

    @when(odd == 1, c >= 4, c < 6, top)
    def _():
        for j in range(1, 8):
            greet(peer(j), block(-1))

    @when(inner_top)
    def _():
        greet(c, block(2))

        @pl.when(even)
        def _():
            greet(c, block(3))

    @when(inner_top, odd == 1, c >= 4)
    def _():
        for j in range(1, 8):
            greet(peer(j), block(2))

    @when(bottom)
    def _():
        greet(c, block(COLUMN - 2))
        greet(c, block(-2))

        @pl.when(odd == 1)
        def _():
            greet(c, block(-3))
            for j in range(1, 8):
                greet(peer(j), block(-2))

        @when(odd == 1, jnp.logical_not(last_column))
        def _():
            greet(c, block(COLUMN))


    @when(top, even, jnp.logical_not(last_column))
    def _():
        greet(c, block(COLUMN))
        greet(c, block(COLUMN + 1))

    @when(top, first_column)
    def _():
        greet(c, block(-COLUMN - odd))


    def count(*conditions):
        return functools.reduce(jnp.logical_and, conditions).astype(jnp.int32)

    present = 8 + count(odd == 1, inner_bottom) * 4 - count(odd == 1, inner_bottom, c >= 4)
    present += count(top, odd == 1) * 7
    present += count(bottom, odd == 1, jnp.logical_not(first_column))
    present += count(even, top) * 2 - count(even, top, c >= 4, c < 6)
    present += count(inner_bottom) * (1 + odd)
    present += count(top) * (3 - odd) + count(top, jnp.logical_not(first_column))
    present += count(top, even, last_column) * 2
    pl.semaphore_wait(barrier, present)

    def answer(dp, cells=c):
        pl.semaphore_signal(late, inc=1, device_id=(cells, dp), device_id_type=MESH)

    @when(odd == 1, inner_bottom)
    def _():
        answer(block(-2))

    @when(top)
    def _():
        answer(block(2 - COLUMN))

        @pl.when(even)
        def _():
            answer(block(2))
            answer(block(3))

        @pl.when(odd == 1)
        def _():
            for j in range(8):
                answer(block(2), peer(j))

    @when(bottom, odd == 1, jnp.logical_not(first_column))
    def _():
        answer(block(-COLUMN))

    @when(top, even, last_column)
    def _():
        answer(block(COLUMN))
        answer(block(COLUMN + 1))

    def copy(source, target, send, recv, cells, dp):
        return pltpu.make_async_remote_copy(
            src_ref=source, dst_ref=target, send_sem=send, recv_sem=recv,
            device_id=(cells, dp), device_id_type=MESH,
        )

    def coef_copy(j):
        return copy(
            gathered.at[c], gathered.at[c], coef_send.at[j - 1], coef_recv.at[c], peer(j), d
        )

    def in_copy(group, j):
        to = peer(j)
        return copy(
            sens.at[rows_of(group, to), :], slab_in.at[c, slab_rows(group), :],
            in_send.at[group, j - 1], in_recv.at[group, c], to, d,
        )

    for one in own[:3]:
        one.wait()
    for j in range(1, 8):
        coef_copy(j).start()
    for group in range(GROUPS):
        for j in range(1, 8):
            in_copy(group, j).start()

    own[3].wait()
    lane = lax.broadcasted_iota(jnp.int32, (GROUP, CZ), 1)
    line = lax.broadcasted_iota(jnp.int32, (GROUP, CZ), 0)
    chosen = lane == line + c * GROUP

    def arrived(buffer, sem, s):
        return copy(buffer.at[s], buffer.at[s], sem.at[s], sem.at[s], c, d)

    for j in range(1, 8):
        arrived(gathered, coef_recv, peer(j)).wait_recv()
    inner = lax.broadcasted_iota(jnp.int32, (8, CZ), 1) < CZ - 1
    for s in range(8):
        if s < 7:
            coef[s, 0:8, :] = gathered[s, 0:8, :]
        else:
            coef[s, 0:4, :] = gathered[s, 0:4, :]
            coef[s, 4:8, :] = jnp.zeros((4, CZ), jnp.float32)
        coef[s, 8:16, :] = gathered[s, 8:16, :]
        coef[s, 16:24, :] = jnp.where(inner, gathered[s, 16:24, :], 0.0)
    def out_copy(group, j):
        to = peer(j)
        return copy(
            slab_out.at[to, slab_rows(group), :], panels.at[PANEL, rows_of(group, c), :],
            out_send.at[group, j - 1], out_recv.at[group, c], to, d,
        )

    for group in range(GROUPS):
        part_rows = slab_rows(group)
        scaled = jnp.sum(
            jnp.where(chosen, weights[group : group + 1, :], 0.0), axis=1, keepdims=True
        )
        own[4 + group].wait()
        for j in range(1, 8):
            landed = slab_in.at[peer(j), part_rows, :]
            sem = in_recv.at[group, peer(j)]
            copy(landed, landed, sem, sem, c, d).wait_recv()

        def load_in(part, tile, part_rows=part_rows):
            return slab_in[part, part_rows, pl.ds(tile * CZ, CZ)].astype(jnp.float32)

        def store_field(part, tile, value, part_rows=part_rows):
            field[part, part_rows, pl.ds(tile * CZ, CZ)] = value

        def load_field(part, tile, part_rows=part_rows):
            return field[part, part_rows, pl.ds(tile * CZ, CZ)]

        def store_out(part, tile, value, part_rows=part_rows, scaled=scaled):
            slab_out[part, part_rows, pl.ds(tile * CZ, CZ)] = (scaled * value).astype(jnp.bfloat16)

        smoothing_pass(load_in, coef, store_field)
        smoothing_pass(load_field, coef, store_out)

        for j in range(1, 8):
            out_copy(group, j).start()
        panels[PANEL, rows_of(group, c), :] = slab_out[c, part_rows, :]

    first_to = jnp.where(even, block(-2), block(-1))
    first_slot = jnp.where(even, 1, 0)
    chunk = 8 * rows // CHUNKS

    def piece(slot, s):
        return panels.at[slot, pl.ds(s * chunk, chunk), :]

    def first_copy(s):
        return copy(
            piece(PANEL, s), piece(first_slot, s), a_send.at[s], panel_recv.at[first_slot, s], c, first_to
        )

    def second_copy(s):
        return copy(piece(PANEL, s), piece(0, s), b_send.at[s], panel_recv.at[0, s], c, block(2))

    relay_to = jnp.where(bottom, block(COLUMN - 2), block(2 - COLUMN))
    relayed_to = jnp.where(bottom, block(COLUMN), block(-COLUMN - odd))
    relayed_slot = jnp.where(bottom, 0, 1 + odd)

    def to_relay_copy(s, send):
        return copy(
            piece(PANEL, s), relay.at[s // 2], send.at[s], relay_recv.at[s // 2], c, relay_to
        )

    def relayed_copy(i):
        s = 2 * i + 1
        return copy(
            relay.at[i], piece(relayed_slot, s), relay_send.at[i], panel_recv.at[relayed_slot, s], c, relayed_to
        )

    def third_copy(s):
        return copy(piece(PANEL, s), piece(2, s), edge_send.at[s], panel_recv.at[2, s], c, block(-3))

    def pass_relayed(first=0):
        for i in range(first, CHUNKS // 2):
            arrived(relay, relay_recv, i).wait_recv()
            relayed_copy(i).start()

    pl.when(jnp.logical_and(top, even))(pass_relayed)

    awaited = count(odd == 1, inner_top) + count(bottom) * 2
    awaited += count(bottom, odd == 1) * 8 + count(top, first_column)
    awaited += count(bottom, odd == 1, jnp.logical_not(last_column))

    @pl.when(awaited > 0)
    def _():
        pl.semaphore_wait(late, awaited)

    def passed_copy(s):
        return copy(piece(1, s), piece(1, s), c_send.at[s], panel_recv.at[1, s], c, block(1))

    def panel_arrived(slot, s):
        return copy(
            piece(slot, s), piece(slot, s), panel_recv.at[slot, s], panel_recv.at[slot, s], c, d
        )

    for s in range(CHUNKS):
        group, low = s // 2, s % 2 * 4
        for source in range(low, low + 4):

            @pl.when(c != source)
            def _(group=group, source=source):
                landed = panels.at[PANEL, rows_of(group, source), :]
                sem = out_recv.at[group, source]
                copy(landed, landed, sem, sem, c, d).wait_recv()

        indirect = s % 2 == 1

        down_indirect = jnp.logical_and(jnp.logical_and(bottom, even), indirect)

        up_indirect = functools.reduce(jnp.logical_and, [top, indirect, jnp.logical_not(last_column)])

        @when(odd == 1, up_indirect)
        def _(s=s):
            to_relay_copy(s, b_send).start()

        @when(odd == 1, jnp.logical_not(up_indirect))
        def _(s=s):
            second_copy(s).start()

        @pl.when(down_indirect)
        def _(s=s):
            to_relay_copy(s, a_send).start()

        @pl.when(jnp.logical_not(down_indirect))
        def _(s=s):
            first_copy(s).start()

    own_rows = at_rows(c)

    def tile_copy(t, j):
        to = peer(j)
        return copy(
            tiles.at[t, at_rows(to), :], sums.at[t, c], tile_send.at[t, j - 1], tile_recv.at[t, c], to, d
        )

    def form(left, right, t):
        tiles[t] = lax.dot_general(
            panels[left], panels[right], (((1,), (1,)), ((), ())),
            preferred_element_type=jnp.float32,
        )

    def far_copy(t, half, first, where):
        return copy(
            tiles.at[t, :, pl.ds(half * CZ, CZ)], far.at[c], far_send.at[half], far_recv.at[c], first + half, where
        )

    def far_tile(left, right, t, first, where):
        form(left, right, t)
        for half in range(2):
            far_copy(t, half, first, where).start()

    def across_copy(j):
        to = peer(j)
        return copy(
            tiles.at[3, at_rows(to), :], sums.at[4, c], across_send.at[j], tile_recv.at[4, c], to, block(-2)
        )

    def tile(left, right, t):
        form(left, right, t)
        for j in range(1, 8):
            tile_copy(t, j).start()
        sums[t, c] = tiles[t, own_rows, :]

    def final_copy(t, half, to, where):
        return copy(
            reduced.at[t, half], landing.at[own_rows, :], last_send.at[t, half], last_recv.at[c], to, where
        )

    def on_each_half(t, k, where, act, keep):
        for half in range(2):
            to = 2 * k + half
            if where is None:

                @pl.when(c != to)
                def _(half=half, to=to):
                    act(final_copy(t, half, to, d))

                @pl.when(c == to)
                def _(half=half):
                    keep(half)

            else:
                act(final_copy(t, half, to, where))

    def reduce(t, k, where=None, first=1):
        for j in range(first, 8):
            s = peer(j)
            copy(sums.at[t, s], sums.at[t, s], tile_recv.at[t, s], tile_recv.at[t, s], c, d).wait_recv()
        value = sums[t, 0]
        for s in range(1, 8):
            value = value + sums[t, s]
        value = value * scale
        reduced[t, 0] = value[:, :CZ]
        reduced[t, 1] = value[:, CZ:]

        def keep(half):
            landing[own_rows, :] = reduced[t, half]

        on_each_half(t, k, where, lambda one: one.start(), keep)

    def end(t, k, where=None):
        for j in range(1, 8):
            tile_copy(t, j).wait_send()
        on_each_half(t, k, where, lambda one: one.wait_send(), lambda half: None)

    @pl.when(odd == 1)
    def _():
        for s in range(CHUNKS):
            indirect = jnp.logical_and(s == CHUNKS - 1, bottom)

            @pl.when(indirect)
            def _(s=s):
                to_relay_copy(s, edge_send).start()

            @pl.when(jnp.logical_not(indirect))
            def _(s=s):
                third_copy(s).start()

    tile(PANEL, PANEL, 0)

    @pl.when(even)
    def _():
        for s in range(CHUNKS):
            panel_arrived(0, s).wait_recv()
        tile(PANEL, 0, 1)
        for s in range(CHUNKS):
            panel_arrived(1, s).wait_recv()
            passed_copy(s).start()
        tile(PANEL, 1, 2)
        reduce(0, 0)
        reduce(1, 1)
        for s in range(CHUNKS):
            panel_arrived(2, s).wait_recv()
        tile(PANEL, 2, 3)

        @pl.when(top)
        def _():
            far_tile(0, 2, 4, 4, block(1))

        reduce(2, 2)
        reduce(3, 3)

    @pl.when(odd == 1)
    def _():

        pl.when(top)(functools.partial(pass_relayed, CHUNKS // 2 - 1))

        @pl.when(inner_bottom)
        def _():
            for s in range(CHUNKS):
                panel_arrived(0, s).wait_recv()
            tile(0, PANEL, 2)

        for s in range(CHUNKS):
            panel_arrived(1, s).wait_recv()

        @pl.when(bottom)
        def _():
            tile(PANEL, 1, 1)
            pl.when(jnp.logical_not(last_column))(pass_relayed)
            reduce(0, 0)
            reduce(1, 1)
            for s in range(CHUNKS):
                panel_arrived(0, s).wait_recv()
            form(0, 1, 3)
            for j in range(8):
                across_copy(j).start()

        @pl.when(inner_bottom)
        def _():
            tile(PANEL, 1, 1)
            tile(0, 1, 3)
            reduce(0, 0)
            reduce(1, 1)
            reduce(2, 2, block(-2))
            reduce(3, 3, block(-2))

        @pl.when(top)
        def _():
            reduce(4, 3, first=0)

    from_far = functools.reduce(jnp.logical_and, [top, odd == 1, c >= 4, c < 6])

    @pl.when(from_far)
    def _():
        for s in range(8):
            arrived(far, far_recv, s).wait_recv()
        value = far[0]
        for s in range(1, 8):
            value = value + far[s]
        landing[...] = value * scale

    @pl.when(jnp.logical_not(from_far))
    def _():
        def landed(s):
            part = landing.at[at_rows(s), :]
            return copy(part, part, last_recv.at[s], last_recv.at[s], c, d)

        for j in range(1, 8):
            landed(peer(j)).wait_recv()

        @when(odd == 1, c >= 4, inner_top)
        def _():
            landed(c).wait_recv()


    final = pltpu.make_async_copy(landing, out, own_sem.at[0])
    final.start()

    for j in range(1, 8):
        coef_copy(j).wait_send()
        for group in range(GROUPS):
            in_copy(group, j).wait_send()
            out_copy(group, j).wait_send()
    for s in range(CHUNKS):
        first_copy(s).wait_send()
    end(0, 0)
    end(1, 1)

    @when(bottom, odd == 1, jnp.logical_not(last_column))
    def _():
        for i in range(CHUNKS // 2):
            relayed_copy(i).wait_send()

    @when(top)
    def _():
        relayed_copy(CHUNKS // 2 - 1).wait_send()

        @pl.when(even)
        def _():
            for i in range(CHUNKS // 2 - 1):
                relayed_copy(i).wait_send()

    @pl.when(even)
    def _():
        for s in range(CHUNKS):
            passed_copy(s).wait_send()
        end(2, 2)
        end(3, 3)

        @pl.when(top)
        def _():
            for half in range(2):
                far_copy(4, half, 4, block(1)).wait_send()

    @pl.when(odd == 1)
    def _():
        for s in range(CHUNKS):
            second_copy(s).wait_send()
            third_copy(s).wait_send()

        @pl.when(inner_bottom)
        def _():
            end(2, 2, block(-2))
            end(3, 3, block(-2))

        @pl.when(bottom)
        def _():
            for j in range(8):
                across_copy(j).wait_send()

        @pl.when(top)
        def _():
            on_each_half(4, 3, None, lambda one: one.wait_send(), lambda half: None)

    final.wait()


def body(sensitivity, weights, coef_x, coef_y, coef_z):
    rows, cells = sensitivity.shape
    part = rows // 8
    scale = float(cells * lax.axis_size("cells")) ** (-0.5)
    dma = pltpu.SemaphoreType.DMA
    return pl.pallas_call(
        functools.partial(kernel, scale),
        out_shape=jax.ShapeDtypeStruct((rows, rows // 2), jnp.float32),
        in_specs=[pl.BlockSpec(memory_space=pl.ANY)] * 5,
        out_specs=pl.BlockSpec(memory_space=pl.ANY),
        scratch_shapes=[
            pltpu.VMEM((2, CZ), jnp.float32),
            pltpu.VMEM((8, 24, CZ), jnp.float32),
            pltpu.VMEM((8, 24, CZ), jnp.float32),
            pltpu.VMEM((8, part, cells), jnp.bfloat16),
            pltpu.VMEM((8, part, cells), jnp.float32),
            pltpu.VMEM((8, part, cells), jnp.bfloat16),
            pltpu.VMEM((4, rows, cells), jnp.bfloat16),
            pltpu.VMEM((5, rows, rows), jnp.float32),
            pltpu.VMEM((5, 8, part, rows), jnp.float32),
            pltpu.VMEM((5, 2, part, CZ), jnp.float32),
            pltpu.VMEM((rows, CZ), jnp.float32),
            pltpu.VMEM((8, rows, CZ), jnp.float32),
            pltpu.VMEM((CHUNKS // 2, rows // CHUNKS, cells), jnp.bfloat16),
            dma((7,)), dma((8,)), dma((GROUPS, 7)), dma((GROUPS, 8)), dma((4 + GROUPS,)), dma((GROUPS, 7)), dma((GROUPS, 8)),
            dma((CHUNKS,)), dma((CHUNKS,)), dma((CHUNKS,)), dma((3, CHUNKS)), dma((4, 7)), dma((5, 8)), dma((5, 2)), dma((8,)),
            dma((CHUNKS // 2,)), dma((CHUNKS // 2,)), pltpu.SemaphoreType.REGULAR, dma((CHUNKS,)), dma((8,)), dma((2,)), dma((8,)),
        ],
        compiler_params=pltpu.CompilerParams(
            collective_id=0, has_side_effects=True, vmem_limit_bytes=60 * 1024 * 1024
        ),
        name="gram_band",
    )(
        sensitivity,
        weights.reshape(2, CZ),
        coef_x.reshape(8, CZ),
        coef_y.reshape(8, CZ),
        coef_z.reshape(8, CZ),
    )


def solution(mesh):
    return jax.shard_map(
        body,
        mesh=mesh,
        in_specs=(P("dp", "cells"), P("dp"), P("cells"), P("cells"), P("cells")),
        out_specs=P("dp", "cells"),
        check_vma=False,
    )
```
